128 devices in a mesh: dp: 16 (over x_lo, y, core), tensor: 8 (over z, x_hi).
Axes of the slice: x: 4 (x_hi: 2, x_lo: 2; x = x_hi * 2 + x_lo), y: 4, z: 4, core: 2. Of those that a mesh axis runs over, the one named last changes fastest.
Arguments:
- tokens: bfloat16 [4096, 6144], P('dp', 'tensor'), may hold values from -6 to 6
- blocks: bfloat16 [4, 6144, 3072], P(None, 'tensor'), may hold values from -0.109375 to 0.109375
- left_factor: bfloat16 [6144, 256], P('tensor'), may hold values from -0.078125 to 0.078125
- right_factor: bfloat16 [256, 24576], P(None, 'tensor'), may hold values from -0.375 to 0.375
- upstream: bfloat16 [4096, 24576], P('dp', 'tensor'), may hold values from -6 to 6
Outputs:
- activated: bfloat16 [4096, 24576], P('dp', 'tensor')
- token_grad: bfloat16 [4096, 6144], P('dp', 'tensor')
- left_grad: bfloat16 [6144, 256], P('tensor')
- right_grad: bfloat16 [256, 24576], P(None, 'tensor')
The draws below stay inside these ranges and needn't reach their ends.
All inputs are finite; a program needn't handle non-finite values.
Results may differ from the reference program's by a relative error of at most 0.0063.
Values may be sent and summed in bfloat16 or wider, within the bound.
A program may use at most 128 MiB of HBM per device.

```python
import jax
import jax.numpy as jnp

DB = 768
FB = 3072
R = 256
SOURCES = 4
D = 6144
FF = 24576
TOKENS = 4096
N_TENSOR = 8


def level_of(rng, extent, pieces, low, top_value):
    level = 1.0
    for axis_at, shards_of in pieces:
        draws = jax.random.uniform(jax.random.fold_in(jax.random.fold_in(rng, 6), axis_at), (shards_of,), jnp.float32, low / len(pieces), top_value / len(pieces))
        level = level * jnp.repeat(jnp.exp(draws), extent[axis_at] // shards_of).reshape((-1,) + (1,) * (len(extent) - 1 - axis_at))
    return level


def gaussian(stream_key, extent, deviation, limit, split=(), held_as=jnp.bfloat16):
    values = deviation * jax.random.normal(stream_key, extent, jnp.float32)
    if split:
        values = values * level_of(stream_key, extent, split, -0.22, 0.18)
    return jnp.clip(values, -limit, limit).astype(held_as)


def setup_inputs(seed: int = 0) -> dict:
    key_list = jax.random.split(jax.random.key(seed), 6)
    return {
        "tokens": gaussian(key_list[0], (TOKENS, D), 1.0, 6.0, ((0, 16), (1, 8))),
        "blocks": gaussian(key_list[1], (SOURCES, D, FB), (SOURCES * DB) ** -0.5, 0.109375, ((1, 8),)),
        "left_factor": gaussian(key_list[2], (D, R), D ** -0.5, 0.078125, ((0, 8),)),
        "right_factor": gaussian(key_list[3], (R, FF), R ** -0.5, 0.375, ((1, 8),)),
        "upstream": gaussian(key_list[4], (TOKENS, FF), 1.0, 6.0, ((0, 16), (1, 8))),
    }


def reference(tokens, blocks, left_factor, right_factor, upstream):
    block_count = N_TENSOR
    levels = blocks.shape[0] - 1
    slabs = tokens.reshape(TOKENS, block_count, DB)
    weights = blocks.reshape(levels + 1, block_count, DB, FB)
    low_rank = jnp.dot(tokens, left_factor, preferred_element_type=jnp.float32).astype(jnp.bfloat16)
    expanded = jnp.dot(low_rank, right_factor, preferred_element_type=jnp.float32).reshape(TOKENS, block_count, FB)
    outputs = []
    for column in range(block_count):
        running = expanded[:, column]
        for section in range(levels + 1):
            source = column if section == 0 else column ^ 1 << section - 1
            running = running + jnp.dot(slabs[:, source], weights[section, column], preferred_element_type=jnp.float32)
        outputs.append(running)
    preact = jnp.stack(outputs, 1).reshape(TOKENS, FF)
    gelu_out, pullback = jax.vjp(jax.nn.gelu, preact)
    activated = gelu_out.astype(jnp.bfloat16)
    slopes = pullback(upstream.astype(jnp.float32))[0].astype(jnp.bfloat16)
    mixed_rows = jnp.dot(slopes, right_factor.T, preferred_element_type=jnp.float32).astype(jnp.bfloat16)
    slope_blocks = slopes.reshape(TOKENS, block_count, FB)
    left_blocks = left_factor.reshape(block_count, DB, R)
    grads = []
    for source in range(block_count):
        running = jnp.dot(mixed_rows, left_blocks[source].T, preferred_element_type=jnp.float32)
        for section in range(levels + 1):
            column = source if section == 0 else source ^ 1 << section - 1
            running = running + jnp.dot(slope_blocks[:, column], weights[section, column].T, preferred_element_type=jnp.float32)
        grads.append(running)
    token_grad = jnp.stack(grads, 1).reshape(TOKENS, D).astype(jnp.bfloat16)
    norm_scale = 1.0 / jnp.sqrt(jnp.float32(TOKENS))
    left_grad = (jnp.dot(tokens.T, mixed_rows, preferred_element_type=jnp.float32) * norm_scale).astype(jnp.bfloat16)
    right_grad = (jnp.dot(low_rank.T, slopes, preferred_element_type=jnp.float32) * norm_scale).astype(jnp.bfloat16)
    return (activated, token_grad, left_grad, right_grad)
```

```python
import functools

import jax
import jax.numpy as jnp
from jax import lax
from jax.experimental import pallas as pl
from jax.experimental.pallas import tpu as pltpu
from jax.sharding import PartitionSpec as P

MESH = pl.DeviceIdType.MESH
BF = jnp.bfloat16
F32 = jnp.float32
C0 = 0.7978845608028654
C1 = 0.044715

NC = 6
NK = 3


def flip(v, mask):
    for b in range(3):
        if mask >> b & 1:
            bit = lax.rem(lax.div(v, 1 << b), 2)
            v = v + (1 - 2 * bit) * (1 << b)
    return v


def mm(a, b):
    return jnp.dot(a, b, preferred_element_type=F32)


def mm_t(a, b):
    return lax.dot_general(a, b, (((1,), (1,)), ((), ())), preferred_element_type=F32)


def kernel(scale, sizes, tok_h, blk_h, lf_h, rf_h, up_h, act_h, tg_h, lg_h, rg_h,
           blk, tok, tok_t, lf, rf, up, act, pre, slo,
           lowf, lowp, low_rs, low, low_t,
           mixf, mixp, mix_rs, mix,
           gs, gr, own,
           rp, rpair, rps, ryr, rys, rxr, rg,
           lp, lpair, lps, l7r, lg,
           load_sem, out_sem, send_sem, recv_sem):
    rows, db, fb, rank = sizes
    cw, kw = fb // NC, db // NK
    part = rows // 8
    hr = rows // 2
    d = lax.axis_index("dp")
    t = lax.axis_index("tensor")
    core = lax.rem(d, 2)
    y = lax.rem(lax.div(d, 2), 4)
    xl = lax.div(d, 8)

    def dev(x, yy, c):
        return (x * 8 + yy * 2 + c, t)

    def peer(mask):
        return (d, flip(t, mask))

    pair = dev(xl, y, 1 - core)
    xpeer = dev(1 - xl, y, core)

    def ypeer(k):
        return dev(xl, lax.rem(y + k, 4), core)

    chips = [(k, f) for f in range(2) for k in range(4) if (k, f) != (0, 0)]

    def chip(k, f):
        return dev(xl if f == 0 else 1 - xl, lax.rem(y + k, 4), core)

    started = []

    def send(src, dst, to):
        i = len(started)
        c = pltpu.make_async_remote_copy(
            src_ref=src, dst_ref=dst, send_sem=send_sem.at[i], recv_sem=recv_sem.at[i],
            device_id=to, device_id_type=MESH)
        c.start()
        started.append(c)
        return c

    loads = []

    def load(src, dst):
        c = pltpu.make_async_copy(src, dst, load_sem.at[len(loads)])
        c.start()
        loads.append(c)
        return c

    outs = []

    def put(src, dst):
        c = pltpu.make_async_copy(src, dst, out_sem.at[len(outs)])
        c.start()
        outs.append(c)

    l_tok = load(tok_h, tok.at[0])
    l_lf = load(lf_h, lf)
    l_blk = [load(blk_h.at[0], blk.at[0])]
    l_rf = load(rf_h, rf)
    l_blk += [load(blk_h.at[s], blk.at[s]) for s in (2, 1)]
    l_blk += [load(blk_h.at[3], blk.at[3])]
    l_up = load(up_h, up)

    bar = pltpu.get_barrier_semaphore()
    peers = [peer(m) for m in range(1, 8)] + [pair] + [chip(k, f) for k, f in chips]
    for p in peers:
        pl.semaphore_signal(bar, inc=1, device_id=p, device_id_type=MESH)

    l_tok.wait()
    l_lf.wait()
    lowf[...] = mm(tok[0], lf[...])
    lowp[...] = lowf[...].astype(BF)
    pl.semaphore_wait(bar, len(peers))

    def scatter(src, dst):
        return [send(src.at[pl.ds(flip(t, m) * part, part)], dst.at[m - 1], peer(m))
                for m in range(1, 8)]

    def gather(buf):
        here = pl.ds(t * part, part)
        return [send(buf.at[here], buf.at[here], peer(m)) for m in range(1, 8)]

    def gather_sum(f32_ref, recv):
        here = pl.ds(t * part, part)
        total = f32_ref[here, :]
        for m in range(7):
            total = total + recv[m].astype(F32)
        return total.astype(BF)

    c_low = scatter(lowp, low_rs)
    quads = [(k, h) for k in range(NK) for h in range(2)]

    def piece(s, k, h):
        return tok.at[s, pl.ds(h * hr, hr), pl.ds(k * kw, kw)]

    c_z1, c_xh = [], []
    for k, h in quads:
        c_z1.append(send(piece(0, k, h), piece(2, k, h), peer(2)))
        c_xh.append(send(piece(0, k, h), piece(1, k, h), peer(1)))

    l_blk[0].wait()

    def col(c):
        return pl.ds(pl.multiple_of(c * cw, cw), cw)

    def own_step(c, _):
        pre[:, col(c)] = mm(tok[0], blk[0, :, col(c)])
        return 0

    lax.fori_loop(0, NC, own_step, 0, unroll=True)
    tok_t[...] = tok[0].astype(F32).T.astype(BF)

    c_z2 = []

    def relay(i):
        k, h = quads[i]
        c_z1[i].wait_recv()
        c_z2.append(send(piece(2, k, h), piece(3, k, h), peer(6)))

    def add_k(s, k):
        ks = pl.ds(k * kw, kw)

        def step(c, _):
            pre[:, col(c)] += mm(tok[s, :, ks], blk[s, ks, col(c)])
            return 0

        lax.fori_loop(0, NC, step, 0, unroll=True)

    relay(0)
    for c in c_low:
        c.wait_recv()
    low[pl.ds(t * part, part), :] = gather_sum(lowf, low_rs)
    c_low_ag = gather(low)
    relay(1)
    l_blk[1].wait()
    add_k(2, 0)
    relay(2)
    l_blk[2].wait()
    c_xh[0].wait_recv()
    c_xh[1].wait_recv()
    add_k(1, 0)
    relay(3)
    add_k(2, 1)
    relay(4)
    c_xh[2].wait_recv()
    c_xh[3].wait_recv()
    add_k(1, 1)
    relay(5)
    add_k(2, 2)
    l_blk[3].wait()
    c_z2[0].wait_recv()
    c_z2[1].wait_recv()
    add_k(3, 0)
    c_xh[4].wait_recv()
    c_xh[5].wait_recv()
    add_k(1, 2)
    l_rf.wait()
    for c in c_low_ag:
        c.wait_recv()
    low_t[...] = low[...].astype(F32).T.astype(BF)

    def low_step(c, _):
        pre[:, col(c)] += mm(low[...], rf[:, col(c)])
        return 0

    lax.fori_loop(0, NC, low_step, 0, unroll=True)
    c_z2[2].wait_recv()
    c_z2[3].wait_recv()
    add_k(3, 1)
    l_up.wait()
    c_z2[4].wait_recv()
    c_z2[5].wait_recv()

    q = rank // 8
    e = rank // 16
    half = rank // 2
    c_pair, c_y, c_x, c_ax, c_ay, c_ap = {}, {}, {}, {}, {}, {}
    base = core * half + y * q

    def r_pair(c):
        c_pair[c] = send(rp.at[c, pl.ds((1 - core) * half, half)], rpair.at[c], pair)

    def r_y(c):
        c_pair[c].wait_recv()
        rps[c] = (rp[c, pl.ds(core * half, half)].astype(F32) + rpair[c].astype(F32)).astype(BF)
        c_y[c] = [send(rps.at[c, pl.ds(lax.rem(y + k, 4) * q, q)], ryr.at[c, k - 1], ypeer(k))
                  for k in (2, 1, 3)]

    def r_x(c):
        for s in c_y[c]:
            s.wait_recv()
        total = rps[c, pl.ds(y * q, q)].astype(F32)
        for k in range(3):
            total = total + ryr[c, k].astype(F32)
        rys[c] = total.astype(BF)
        c_x[c] = send(rys.at[c, pl.ds((1 - xl) * e, e)], rxr.at[c], xpeer)

    def r_ax(c):
        c_x[c].wait_recv()
        total = rys[c, pl.ds(xl * e, e)].astype(F32) + rxr[c].astype(F32)
        here = pl.ds(base + xl * e, e)
        rg[c, here] = (total * scale).astype(BF)
        c_ax[c] = send(rg.at[c, here], rg.at[c, here], xpeer)

    def r_ay(c):
        c_ax[c].wait_recv()
        here = pl.ds(base, q)
        c_ay[c] = [send(rg.at[c, here], rg.at[c, here], ypeer(k)) for k in (2, 1, 3)]

    def r_ap(c):
        for s in c_ay[c]:
            s.wait_recv()
        here = pl.ds(core * half, half)
        c_ap[c] = send(rg.at[c, here], rg.at[c, here], pair)

    def r_out(c):
        c_ap[c].wait_recv()
        put(rg.at[c], rg_h.at[:, pl.ds(c * cw, cw)])

    last = pl.ds((NK - 1) * kw, kw)
    for c in range(NC):
        cs = pl.ds(c * cw, cw)
        v = pre[:, cs] + mm(tok[3, :, last], blk[3, last, cs])
        u = up[:, cs].astype(F32)
        v2 = v * v
        th = jnp.tanh(v * (C0 + (C0 * C1) * v2))
        g = 0.5 + 0.5 * th
        act[:, cs] = (v * g).astype(BF)
        slope = g + 0.5 * v * (1.0 - th * th) * (C0 + (3.0 * C0 * C1) * v2)
        sl = (u * slope).astype(BF)
        slo[:, cs] = sl
        put(act.at[:, cs], act_h.at[:, cs])
        rp[c] = mm(low_t[...], sl).astype(BF)
        r_pair(c)
        m = mm_t(sl, rf[:, cs])
        if c == 0:
            mixf[...] = m
        else:
            mixf[...] += m
        if c >= 3:
            r_y(c - 3)
    mixp[...] = mixf[...].astype(BF)
    c_mix = scatter(mixp, mix_rs)

    def back(s, k):
        return mm_t(slo[...], blk[s, pl.ds(k * kw, kw), :])

    def gcol(ref, i, k):
        return ref.at[i, :, pl.ds(k * kw, kw)]

    c_g2, c_gx, c_g1 = [], [], []
    for k in range(NK):
        gs[0, :, pl.ds(k * kw, kw)] = back(3, k).astype(BF)
        c_g2.append(send(gcol(gs, 0, k), gcol(gr, 0, k), peer(6)))
        r_y(NC - 3 + k)
    for k in range(NK):
        gs[1, :, pl.ds(k * kw, kw)] = back(1, k).astype(BF)
        c_gx.append(send(gcol(gs, 1, k), gcol(gr, 1, k), peer(1)))
    r_x(0)
    for c in c_mix:
        c.wait_recv()
    mix[pl.ds(t * part, part), :] = gather_sum(mixf, mix_rs)
    c_mix_ag = gather(mix)
    for k in range(NK):
        ks = pl.ds(k * kw, kw)
        p = back(2, k)
        c_g2[k].wait_recv()
        gs[2, :, ks] = (p + gr[0, :, ks].astype(F32)).astype(BF)
        c_g1.append(send(gcol(gs, 2, k), gcol(gr, 2, k), peer(2)))
        r_x(1 + k)
        r_ax(k)
    for k in range(NK):
        own[:, pl.ds(k * kw, kw)] = back(0, k)
    r_ay(0)
    r_x(4)
    r_ax(3)
    r_ay(1)

    for c in c_mix_ag:
        c.wait_recv()
    lp[...] = mm(tok_t[...], mix[...]).astype(BF)
    lh, le = db // 2, db // 16
    c_lpair = send(lp.at[pl.ds((1 - core) * lh, lh)], lpair, pair)
    r_ay(2)
    r_x(5)
    r_ax(4)
    c_lpair.wait_recv()
    lps[...] = (lp[pl.ds(core * lh, lh)].astype(F32) + lpair[...].astype(F32)).astype(BF)
    c_l7 = []
    for i, (k, f) in enumerate(chips):
        xx = xl if f == 0 else 1 - xl
        at = lax.rem(y + k, 4) * (2 * le) + xx * le
        c_l7.append(send(lps.at[pl.ds(at, le)], l7r.at[i], chip(k, f)))
    r_ay(3)
    r_ax(5)
    r_ap(0)
    r_ap(1)
    r_ay(4)
    for k in range(NK):
        own[:, pl.ds(k * kw, kw)] += mm_t(mix[...], lf[pl.ds(k * kw, kw), :])
    r_out(0)
    r_ap(2)
    for c in c_l7:
        c.wait_recv()
    total = lps[pl.ds(y * (2 * le) + xl * le, le)].astype(F32)
    for i in range(7):
        total = total + l7r[i].astype(F32)
    here = pl.ds(core * lh + y * (2 * le) + xl * le, le)
    lg[here] = (total * scale).astype(BF)
    c_lag = [send(lg.at[here], lg.at[here], chip(k, f)) for k, f in chips]
    r_ay(5)
    r_ap(3)
    for k in range(NK):
        ks = pl.ds(k * kw, kw)
        c_gx[k].wait_recv()
        c_g1[k].wait_recv()
        tok[1, :, ks] = (own[:, ks] + gr[1, :, ks].astype(F32) + gr[2, :, ks].astype(F32)).astype(BF)
    put(tok.at[1], tg_h)
    r_out(1)
    r_ap(4)
    r_out(2)
    for c in c_lag:
        c.wait_recv()
    here = pl.ds(core * lh, lh)
    c_lap = send(lg.at[here], lg.at[here], pair)
    r_ap(5)
    r_out(3)
    r_out(4)
    c_lap.wait_recv()
    put(lg, lg_h)
    r_out(5)
    for c in started:
        c.wait_send()
    for c in outs:
        c.wait()


def move(*refs):
    n = (len(refs) - 1) // 2
    sem = refs[-1]
    cs = [pltpu.make_async_copy(refs[i], refs[n + i], sem.at[i]) for i in range(n)]
    for c in cs:
        c.start()
    for c in cs:
        c.wait()


def body(scale, tokens, blocks, left_factor, right_factor, upstream):
    rows, db = tokens.shape
    ns, _, fb = blocks.shape
    rank = left_factor.shape[1]
    cw = fb // NC
    part = rows // 8
    shapes = [
        jax.ShapeDtypeStruct((rows, fb), BF),
        jax.ShapeDtypeStruct((rows, db), BF),
        jax.ShapeDtypeStruct((db, rank), BF),
        jax.ShapeDtypeStruct((rank, fb), BF),
    ]
    V = pltpu.VMEM
    scratch = [
        V((ns, db, fb), BF), V((ns, rows, db), BF), V((db, rows), BF), V((db, rank), BF),
        V((rank, fb), BF), V((rows, fb), BF), V((rows, fb), BF), V((rows, fb), F32), V((rows, fb), BF),
        V((rows, rank), F32), V((rows, rank), BF), V((7, part, rank), BF), V((rows, rank), BF), V((rank, rows), BF),
        V((rows, rank), F32), V((rows, rank), BF), V((7, part, rank), BF), V((rows, rank), BF),
        V((3, rows, db), BF), V((3, rows, db), BF), V((rows, db), F32),
        V((NC, rank, cw), BF), V((NC, rank // 2, cw), BF), V((NC, rank // 2, cw), BF),
        V((NC, 3, rank // 8, cw), BF), V((NC, rank // 8, cw), BF), V((NC, rank // 16, cw), BF), V((NC, rank, cw), BF),
        V((db, rank), BF), V((db // 2, rank), BF), V((db // 2, rank), BF), V((7, db // 16, rank), BF), V((db, rank), BF),
        pltpu.SemaphoreType.DMA((8,)), pltpu.SemaphoreType.DMA((16,)),
        pltpu.SemaphoreType.DMA((160,)), pltpu.SemaphoreType.DMA((160,)),
    ]
    any_spec = pl.BlockSpec(memory_space=pl.ANY)
    res = pl.pallas_call(
        functools.partial(kernel, scale, (rows, db, fb, rank)),
        out_shape=shapes,
        in_specs=[any_spec] * 5,
        out_specs=[any_spec] * 4,
        scratch_shapes=scratch,
        compiler_params=pltpu.CompilerParams(
            collective_id=0, has_side_effects=True, vmem_limit_bytes=56 * 1024 * 1024
        ),
    )(tokens, blocks, left_factor, right_factor, upstream)
    return pl.pallas_call(
        move,
        out_shape=shapes,
        in_specs=[any_spec] * 4,
        out_specs=[any_spec] * 4,
        scratch_shapes=[pltpu.SemaphoreType.DMA((4,))],
    )(*res)


def solution(mesh):
    placed = (
        P("dp", "tensor"),
        P(None, "tensor", None),
        P("tensor", None),
        P(None, "tensor"),
        P("dp", "tensor"),
    )

    def whole(tokens, blocks, left_factor, right_factor, upstream):
        scale = 1.0 / float(tokens.shape[0]) ** 0.5
        return jax.shard_map(
            functools.partial(body, scale),
            mesh=mesh,
            in_specs=placed,
            out_specs=(P("dp", "tensor"), P("dp", "tensor"), P("tensor", None), P(None, "tensor")),
            check_vma=False,
        )(tokens, blocks, left_factor, right_factor, upstream)

    return whole
```

```python
import functools

import jax
import jax.numpy as jnp
from jax import lax
from jax.experimental import pallas as pl
from jax.experimental.pallas import tpu as pltpu
from jax.sharding import PartitionSpec as P

MESH = pl.DeviceIdType.MESH
BF = jnp.bfloat16
F32 = jnp.float32
C0 = 0.7978845608028654
C1 = 0.044715

NC = 6
NG = 3
XF = (4, 5)
NK = 3


def flip(v, mask):
    for b in range(3):
        if mask >> b & 1:
            bit = lax.rem(lax.div(v, 1 << b), 2)
            v = v + (1 - 2 * bit) * (1 << b)
    return v


def mm(a, b):
    return jnp.dot(a, b, preferred_element_type=F32)


def mm_t(a, b):
    return lax.dot_general(a, b, (((1,), (1,)), ((), ())), preferred_element_type=F32)


def kernel(scale, sizes, tok_h, blk_h, lf_h, rf_h, up_h, act, tg, lg, rg,
           blk, tok, tok_t, lf, rf, up, pre, slo,
           lowf, lowp, low_rs, low, low_t,
           mixf, mixp, mix_rs, mix,
           gs, gr, own,
           rp, rpair, rps, ryr, rys, rxr, rxs,
           lp, lpair, lps, l7r,
           load_sem, send_sem, recv_sem):
    rows, db, fb, rank = sizes
    cw, kw, gw = fb // NC, db // NK, fb // NG
    part = rows // 8
    hr = rows // 2
    d = lax.axis_index("dp")
    t = lax.axis_index("tensor")
    core = lax.rem(d, 2)
    y = lax.rem(lax.div(d, 2), 4)
    xl = lax.div(d, 8)

    def dev(x, yy, c):
        return (x * 8 + yy * 2 + c, t)

    def peer(mask):
        return (d, flip(t, mask))

    def yat(k):
        return lax.rem(y + k, 4)

    pair = dev(xl, y, 1 - core)
    xpeer = dev(1 - xl, y, core)
    chips = [(k, f) for f in range(2) for k in (2, 1, 3, 0) if (k, f) != (0, 0)]

    def chip(k, f):
        return dev(xl if f == 0 else 1 - xl, yat(k), core)

    bar = pltpu.get_barrier_semaphore()
    peers = [peer(m) for m in (7, 5, 6, 4, 3, 1, 2)] + [chip(k, f) for k, f in chips] + [pair]
    for p in peers:
        pl.semaphore_signal(bar, inc=1, device_id=p, device_id_type=MESH)

    loads = []

    def load(src, dst):
        c = pltpu.make_async_copy(src, dst, load_sem.at[len(loads)])
        c.start()
        loads.append(c)
        return c

    l_tok = load(tok_h, tok.at[0])
    l_lf = load(lf_h, lf)
    l_blk = {}
    for i in (0, 2, 1, 3):
        l_blk[i] = load(blk_h.at[i], blk.at[i])
    l_rf = load(rf_h, rf)
    l_up = load(up_h, up)

    groups = []

    class Group:
        def __init__(self, copies, size):
            n = len(groups)
            if n >= N_SEND:
                groups[n - N_SEND].sent()
            self.ssem, self.rsem, self.size, self.open = send_sem.at[n % N_SEND], recv_sem.at[n], size, True
            groups.append(self)
            for src, dst, to in copies:
                pltpu.make_async_remote_copy(
                    src_ref=src, dst_ref=dst, send_sem=self.ssem, recv_sem=self.rsem,
                    device_id=to, device_id_type=MESH).start()

        def got(self):
            pltpu.make_async_copy(self.size, self.size, self.rsem).wait()

        def sent(self):
            if self.open:
                pltpu.make_async_copy(self.size, self.size, self.ssem).wait()
                self.open = False

    def send(src, dst, to):
        return Group([(src, dst, to)], src)

    def scatter(src, dst):
        return Group([(src.at[pl.ds(flip(t, m) * part, part)], dst.at[m - 1], peer(m)) for m in (7, 5, 6, 4, 3, 1, 2)], dst)

    def gather(buf):
        here = buf.at[pl.ds(t * part, part)]
        return Group([(here, here, peer(m)) for m in (7, 5, 6, 4, 3, 1, 2)], buf.at[pl.ds(0, 7 * part)])

    def gather_sum(f32_ref, recv):
        total = f32_ref[pl.ds(t * part, part), :]
        for m in range(7):
            total = total + recv[m].astype(F32)
        return total.astype(BF)

    def col(c):
        return pl.ds(pl.multiple_of(c * cw, cw), cw)

    def add_k(s, k):
        ks = pl.ds(k * kw, kw)

        def step(c, _):
            pre[:, col(c)] += mm(tok[s, :, ks], blk[s, ks, col(c)])
            return 0

        lax.fori_loop(0, NC, step, 0, unroll=True)

    quads = [(k, h) for k in range(NK) for h in range(2)]

    def piece(s, k, h):
        return tok.at[s, pl.ds(h * hr, hr), pl.ds(k * kw, kw)]

    c_z1, c_xh, c_z2 = [], [], []

    def send_tok(i):
        k, h = quads[i]
        c_z1.append(send(piece(0, k, h), piece(2, k, h), peer(2)))
        c_xh.append(send(piece(0, k, h), piece(1, k, h), peer(1)))

    def relay(i):
        k, h = quads[i]
        c_z1[i].got()
        c_z2.append(send(piece(2, k, h), piece(3, k, h), peer(6)))

    def own_fwd():
        l_blk[0].wait()

        def step(c, _):
            pre[:, col(c)] = mm(tok[0], blk[0, :, col(c)])
            return 0

        lax.fori_loop(0, NC, step, 0, unroll=True)
        tok_t[...] = tok[0].astype(F32).T.astype(BF)

    def low_fwd():
        low_t[...] = low[...].astype(F32).T.astype(BF)

        def step(c, _):
            pre[:, col(c)] += mm(low[...], rf[:, col(c)])
            return 0

        lax.fori_loop(0, NC, step, 0, unroll=True)

    st = {}

    def run(name, *a):
        with jax.named_scope(name + "".join("_%d" % i for i in a)):
            OPS[name](*a)

    def start():
        l_tok.wait()
        l_lf.wait()
        lowf[...] = mm(tok[0], lf[...])
        lowp[...] = lowf[...].astype(BF)

    def barrier():
        pl.semaphore_wait(bar, len(peers))

    def low_rs_send():
        st["low"] = scatter(lowp, low_rs)

    def low_ag_send():
        st["low"].got()
        low[pl.ds(t * part, part), :] = gather_sum(lowf, low_rs)
        st["low_ag"] = gather(low)

    def w_low():
        l_rf.wait()
        st["low_ag"].got()

    def w_blk(i):
        l_blk[i].wait()

    def w_xh(k):
        c_xh[2 * k].got()
        c_xh[2 * k + 1].got()

    def w_z2(k):
        c_z2[2 * k].got()
        c_z2[2 * k + 1].got()

    def gelu(c):
        if c == 0:
            l_up.wait()
        cs = pl.ds(c * gw, gw)
        v = pre[:, cs]
        u = up[:, cs].astype(F32)
        v2 = v * v
        th = jnp.tanh(v * (C0 + (C0 * C1) * v2))
        g = 0.5 + 0.5 * th
        act[:, cs] = (v * g).astype(BF)
        slope = g + 0.5 * v * (1.0 - th * th) * (C0 + (3.0 * C0 * C1) * v2)
        slo[:, cs] = (u * slope).astype(BF)
        n = NC // NG
        for i in range(n):
            rp[c * n + i] = mm(low_t[...], slo[:, pl.ds(c * gw + i * cw, cw)]).astype(BF)
        for i in range(n):
            r_pair(c * n + i)

    def mix_send():
        mixf[...] = mm_t(slo[...], rf[...])
        mixp[...] = mixf[...].astype(BF)
        st["mix"] = scatter(mixp, mix_rs)

    def mix_ag_send():
        st["mix"].got()
        mix[pl.ds(t * part, part), :] = gather_sum(mixf, mix_rs)
        st["mix_ag"] = gather(mix)

    half, q, e = rank // 2, rank // 8, rank // 16
    g = {}

    def rgc(c, at, n):
        return rg.at[pl.ds(at, n), pl.ds(c * cw, cw)]

    def first(c):
        return (xl * (half // 2), half // 2) if c in XF else (y * q, q)

    def mine(c):
        return core * half + (xl * (half // 2) + y * e if c in XF else y * q + xl * e)

    def r_pair(c):
        g["p", c] = send(rp.at[c, pl.ds((1 - core) * half, half)], rpair.at[c], pair)

    def r_s2(c):
        g["p", c].got()
        rps[c] = (rp[c, pl.ds(core * half, half)].astype(F32) + rpair[c].astype(F32)).astype(BF)
        if c in XF:
            n = half // 2
            g["s2", c] = send(rps.at[c, pl.ds((1 - xl) * n, n)], rxr.at[c, pl.ds(0, n)], xpeer)
        else:
            g["s2", c] = Group([(rps.at[c, pl.ds(yat(k) * q, q)], ryr.at[c, k - 1], (dev(xl, yat(k), core)))
                                for k in (2, 1, 3)], ryr.at[c])

    def r_s3(c):
        g["s2", c].got()
        if c in XF:
            n = half // 2
            rxs[c % 2] = (rps[c, pl.ds(xl * n, n)].astype(F32) + rxr[c, pl.ds(0, n)].astype(F32)).astype(BF)
            g["s3", c] = Group([(rxs.at[c % 2, pl.ds(yat(k) * e, e)], ryr.at[c, k - 1, pl.ds(0, e)], (dev(xl, yat(k), core)))
                                for k in (2, 1, 3)], rps.at[c, pl.ds(0, 3 * e)])
        else:
            total = rps[c, pl.ds(y * q, q)].astype(F32)
            for k in range(3):
                total = total + ryr[c, k].astype(F32)
            rys[c] = total.astype(BF)
            g["s3", c] = send(rys.at[c, pl.ds((1 - xl) * e, e)], rxr.at[c, pl.ds(0, e)], xpeer)

    def r_a1(c):
        g["s3", c].got()
        if c in XF:
            total = rxs[c % 2, pl.ds(y * e, e)].astype(F32)
            for k in range(3):
                total = total + ryr[c, k, pl.ds(0, e)].astype(F32)
        else:
            total = rys[c, pl.ds(xl * e, e)].astype(F32) + rxr[c, pl.ds(0, e)].astype(F32)
        rg[pl.ds(mine(c), e), pl.ds(c * cw, cw)] = (total * scale).astype(BF)
        here = rgc(c, mine(c), e)
        if c in XF:
            g["a1", c] = Group([(here, here, dev(xl, yat(k), core)) for k in (2, 1, 3)], rps.at[c, pl.ds(0, 3 * e)])
        else:
            g["a1", c] = send(here, here, xpeer)

    def r_a2(c):
        g["a1", c].got()
        at, n = first(c)
        here = rgc(c, core * half + at, n)
        if c in XF:
            g["a2", c] = send(here, here, xpeer)
        else:
            g["a2", c] = Group([(here, here, dev(xl, yat(k), core)) for k in (2, 1, 3)], ryr.at[c])

    def r_a3(c):
        g["a2", c].got()
        here = rgc(c, core * half, half)
        g["a3", c] = send(here, here, pair)

    def r_end(c):
        g["a3", c].got()

    def back(s):
        return mm_t(slo[...], blk[s])

    def gcol(ref, i, k, n=NK):
        w = db // n
        return ref.at[i, :, pl.ds(k * w, w)]

    NX = 6

    def p2():
        gs[0] = back(3).astype(BF)
        for k in range(NK):
            g["g2", k] = send(gcol(gs, 0, k), gcol(gr, 0, k), peer(6))

    def px():
        gs[1] = back(1).astype(BF)

    def px_send(k):
        g["gx", k] = send(gcol(gs, 1, k, NX), gcol(gr, 1, k, NX), peer(1))

    def p1():
        pre[:, pl.ds(0, db)] = back(2)

    def p1_send(k):
        ks = pl.ds(k * kw, kw)
        g["g2", k].got()
        gs[2, :, ks] = (pre[:, ks] + gr[0, :, ks].astype(F32)).astype(BF)
        g["g1", k] = send(gcol(gs, 2, k), gcol(gr, 2, k), peer(2))

    def p0():
        own[...] = back(0)

    lh, le = db // 2, db // 16

    def left(i=0):
        st["mix_ag"].got()
        lp[...] = mm(tok_t[...], mix[...]).astype(BF)
        g["lp"] = send(lp.at[pl.ds((1 - core) * lh, lh)], lpair, pair)
        own[...] += mm_t(mix[...], lf[...])

    def left_rs():
        g["lp"].got()
        lps[...] = (lp[pl.ds(core * lh, lh)].astype(F32) + lpair[...].astype(F32)).astype(BF)
        cs = []
        for i, (k, f) in enumerate(chips):
            xx = xl if f == 0 else 1 - xl
            cs.append((lps.at[pl.ds(yat(k) * (2 * le) + xx * le, le)], l7r.at[i], chip(k, f)))
        g["l7"] = Group(cs, l7r)

    def left_ag():
        g["l7"].got()
        at = y * (2 * le) + xl * le
        total = lps[pl.ds(at, le)].astype(F32)
        for i in range(7):
            total = total + l7r[i].astype(F32)
        lg[pl.ds(core * lh + at, le)] = (total * scale).astype(BF)
        here = lg.at[pl.ds(core * lh + at, le)]
        g["la"] = Group([(here, here, chip(k, f)) for k, f in chips], l7r)

    def left_pair():
        g["la"].got()
        here = lg.at[pl.ds(core * lh, lh)]
        g["lap"] = send(here, here, pair)

    def left_end():
        g["lap"].got()

    def tg_end():
        for k in range(NX):
            g["gx", k].got()
        for k in range(NK):
            g["g1", k].got()
        tg[...] = (own[...] + gr[1].astype(F32) + gr[2].astype(F32)).astype(BF)

    def finish():
        for c in groups:
            c.sent()

    OPS = dict(locals())
    for name, *a in ORDER:
        run(name, *a)


ORDER = [
    ("start",), ("barrier",), ("send_tok", 0), ("low_rs_send",),
    *[("send_tok", i) for i in range(1, 6)],
    ("own_fwd",),
    ("relay", 0), ("relay", 1), ("low_ag_send",), ("w_blk", 2), ("add_k", 2, 0),
    ("relay", 2), ("w_blk", 1), ("w_xh", 0), ("add_k", 1, 0), ("relay", 3), ("add_k", 2, 1),
    ("relay", 4), ("w_xh", 1), ("add_k", 1, 1), ("relay", 5), ("add_k", 2, 2),
    ("w_blk", 3), ("w_z2", 0), ("add_k", 3, 0), ("w_xh", 2), ("add_k", 1, 2),
    ("w_low",), ("low_fwd",), ("w_z2", 1), ("add_k", 3, 1), ("w_z2", 2), ("add_k", 3, 2),
    ("gelu", 0), ("gelu", 1), ("gelu", 2),
    ("r_s2", 0), ("r_s2", 1), ("mix_send",), ("r_s2", 2), ("r_s2", 3), ("p2",), ("r_s2", 4), ("r_s2", 5),
    ("px",), ("px_send", 0), ("p1",), ("r_s3", 0), ("px_send", 1), ("mix_ag_send",), ("r_s3", 1), ("px_send", 2),
    ("r_s3", 4), ("r_s3", 5), ("p0",), ("r_a1", 0), ("p1_send", 0), ("r_s3", 2), ("px_send", 3),
    ("r_s3", 3), ("r_a1", 1), ("px_send", 4), ("p1_send", 1), ("r_a2", 0), ("r_a1", 2), ("px_send", 5),
    ("left",), ("r_a2", 1), ("r_a1", 3), ("p1_send", 2), ("left_rs",), ("r_a2", 2),
    ("r_a1", 4), ("r_a1", 5), ("r_a2", 3), ("r_a3", 0), ("r_a3", 1), ("r_a2", 4), ("r_a2", 5),
    ("left_ag",), ("r_a3", 2), ("tg_end",), ("r_a3", 3), ("r_a3", 4), ("r_a3", 5), ("left_pair",),
    *[("r_end", i) for i in range(6)], ("left_end",), ("finish",),
]
N_SEND = 20
N_RECV = 90


def move(*refs):
    n = len(refs) // 2
    sem = refs[-1]
    cs = [pltpu.make_async_copy(refs[i], refs[n + i], sem.at[i]) for i in range(n)]
    for c in cs:
        c.start()
    for c in cs:
        c.wait()


def body(scale, tokens, blocks, left_factor, right_factor, upstream):
    rows, db = tokens.shape
    ns, _, fb = blocks.shape
    rank = left_factor.shape[1]
    cw = fb // NC
    part = rows // 8
    shapes = [
        jax.ShapeDtypeStruct((rows, fb), BF),
        jax.ShapeDtypeStruct((rows, db), BF),
        jax.ShapeDtypeStruct((db, rank), BF),
        jax.ShapeDtypeStruct((rank, fb), BF),
    ]
    V = pltpu.VMEM
    scratch = [
        V((ns, db, fb), BF), V((ns, rows, db), BF), V((db, rows), BF), V((db, rank), BF),
        V((rank, fb), BF), V((rows, fb), BF), V((rows, fb), F32), V((rows, fb), BF),
        V((rows, rank), F32), V((rows, rank), BF), V((7, part, rank), BF), V((rows, rank), BF), V((rank, rows), BF),
        V((rows, rank), F32), V((rows, rank), BF), V((7, part, rank), BF), V((rows, rank), BF),
        V((3, rows, db), BF), V((3, rows, db), BF), V((rows, db), F32),
        V((NC, rank, cw), BF), V((NC, rank // 2, cw), BF), V((NC, rank // 2, cw), BF),
        V((NC, 3, rank // 8, cw), BF), V((NC, rank // 8, cw), BF), V((NC, rank // 4, cw), BF), V((2, rank // 4, cw), BF),
        V((db, rank), BF), V((db // 2, rank), BF), V((db // 2, rank), BF), V((7, db // 16, rank), BF),
        pltpu.SemaphoreType.DMA((8,)), pltpu.SemaphoreType.DMA((N_SEND,)), pltpu.SemaphoreType.DMA((N_RECV,)),
    ]
    any_spec = pl.BlockSpec(memory_space=pl.ANY)
    vmem_spec = pl.BlockSpec(memory_space=pltpu.VMEM)
    res = pl.pallas_call(
        functools.partial(kernel, scale, (rows, db, fb, rank)),
        out_shape=[V(o.shape, o.dtype) for o in shapes],
        in_specs=[any_spec] * 5,
        out_specs=[vmem_spec] * 4,
        scratch_shapes=scratch,
        compiler_params=pltpu.CompilerParams(
            collective_id=0, has_side_effects=True, vmem_limit_bytes=56 * 1024 * 1024
        ),
    )(tokens, blocks, left_factor, right_factor, upstream)
    return pl.pallas_call(
        move,
        out_shape=shapes,
        in_specs=[vmem_spec] * 4,
        out_specs=[any_spec] * 4,
        scratch_shapes=[pltpu.SemaphoreType.DMA((4,))],
        compiler_params=pltpu.CompilerParams(vmem_limit_bytes=1024 * 1024),
    )(*[pltpu.with_memory_space_constraint(r, pltpu.VMEM) for r in res])


def solution(mesh):
    placed = (
        P("dp", "tensor"),
        P(None, "tensor", None),
        P("tensor", None),
        P(None, "tensor"),
        P("dp", "tensor"),
    )

    def whole(tokens, blocks, left_factor, right_factor, upstream):
        scale = 1.0 / float(tokens.shape[0]) ** 0.5
        return jax.shard_map(
            functools.partial(body, scale),
            mesh=mesh,
            in_specs=placed,
            out_specs=(P("dp", "tensor"), P("dp", "tensor"), P("tensor", None), P(None, "tensor")),
            check_vma=False,
        )(tokens, blocks, left_factor, right_factor, upstream)

    return whole
```

```python
import functools

import jax
import jax.numpy as jnp
from jax import lax
from jax.experimental import pallas as pl
from jax.experimental.pallas import tpu as pltpu
from jax.sharding import PartitionSpec as P

MESH = pl.DeviceIdType.MESH
BF = jnp.bfloat16
F32 = jnp.float32
C0 = 0.7978845608028654
C1 = 0.044715

NC = 6
NG = 3
NK = 3


def flip(v, mask):
    for b in range(3):
        if mask >> b & 1:
            bit = lax.rem(lax.div(v, 1 << b), 2)
            v = v + (1 - 2 * bit) * (1 << b)
    return v


def mm(a, b):
    return jnp.dot(a, b, preferred_element_type=F32)


def mm_t(a, b):
    return lax.dot_general(a, b, (((1,), (1,)), ((), ())), preferred_element_type=F32)


def kernel(scale, sizes, tok_h, blk_h, lf_h, rf_h, up_h, act, tg, lg, rg,
           blk, tok, tok_t, lf, rf, up, pre, slo,
           lowf, lowp, low_rs, low, low_t,
           mixf, mixp, mix_rs, mix,
           rb, gs, gr, own,
           rp, rpair, rps, yrl, yfin, ybs, yb, rys, rxr,
           lp, lpair, lps, l7r,
           load_sem, send_sem, recv_sem):
    rows, db, fb, rank = sizes
    cw, kw, gw = fb // NC, db // NK, fb // NG
    part = rows // 8
    d = lax.axis_index("dp")
    t = lax.axis_index("tensor")
    core = lax.rem(d, 2)
    y = lax.rem(lax.div(d, 2), 4)
    xl = lax.div(d, 8)

    def dev(x, yy, c):
        return (x * 8 + yy * 2 + c, t)

    def peer(mask):
        return (d, flip(t, mask))

    def yat(k):
        return lax.rem(y + k, 4)

    pair = dev(xl, y, 1 - core)
    xpeer = dev(1 - xl, y, core)
    chips = [(k, f) for f in range(2) for k in (2, 1, 3, 0) if (k, f) != (0, 0)]

    def chip(k, f):
        return dev(xl if f == 0 else 1 - xl, yat(k), core)

    bar = pltpu.get_barrier_semaphore()
    peers = [peer(m) for m in (7, 5, 6, 4, 3, 1, 2)] + [chip(k, f) for k, f in chips] + [pair]
    for p in peers:
        pl.semaphore_signal(bar, inc=1, device_id=p, device_id_type=MESH)

    loads = []

    def load(src, dst):
        c = pltpu.make_async_copy(src, dst, load_sem.at[len(loads)])
        c.start()
        loads.append(c)
        return c

    l_tok = load(tok_h, tok.at[0])
    l_lf = load(lf_h, lf)
    l_blk = {}
    for i in (0, 2, 1, 3):
        l_blk[i] = load(blk_h.at[i], blk.at[i])
    l_rf = load(rf_h, rf)
    l_up = load(up_h, up)

    groups = []

    class Group:
        def __init__(self, copies, size):
            n = len(groups)
            if n >= N_SEND:
                groups[n - N_SEND].sent()
            self.ssem, self.rsem, self.size, self.open = send_sem.at[n % N_SEND], recv_sem.at[n], size, True
            groups.append(self)
            for src, dst, to in copies:
                pltpu.make_async_remote_copy(
                    src_ref=src, dst_ref=dst, send_sem=self.ssem, recv_sem=self.rsem,
                    device_id=to, device_id_type=MESH).start()

        def got(self):
            pltpu.make_async_copy(self.size, self.size, self.rsem).wait()

        def sent(self):
            if self.open:
                pltpu.make_async_copy(self.size, self.size, self.ssem).wait()
                self.open = False

    def send(src, dst, to):
        return Group([(src, dst, to)], dst)

    def scatter(src, dst):
        return Group([(src.at[pl.ds(flip(t, m) * part, part)], dst.at[m - 1], peer(m)) for m in (7, 5, 6, 4, 3, 1, 2)], dst)

    def gather(buf):
        here = buf.at[pl.ds(t * part, part)]
        return Group([(here, here, peer(m)) for m in (7, 5, 6, 4, 3, 1, 2)], buf.at[pl.ds(0, 7 * part)])

    def gather_sum(f32_ref, recv):
        total = f32_ref[pl.ds(t * part, part), :]
        for m in range(7):
            total = total + recv[m].astype(F32)
        return total.astype(BF)

    def col(c):
        return pl.ds(pl.multiple_of(c * cw, cw), cw)

    def add_k(s, k):
        ks = pl.ds(k * kw, kw)

        def step(c, _):
            pre[:, col(c)] += mm(tok[s, :, ks], blk[s, ks, col(c)])
            return 0

        lax.fori_loop(0, NC, step, 0, unroll=True)

    hr = rows // NH
    quads = [(k, h) for k in range(NK) for h in range(NH)]

    def piece(s, k, h):
        return tok.at[s, pl.ds(h * hr, hr), pl.ds(k * kw, kw)]

    c_z1, c_xh, c_z2, c_b, c_z2b = [], [], [], [], []

    def send_z(i):
        k, h = quads[i]
        c_z1.append(send(tok_h.at[pl.ds(h * hr, hr), pl.ds(k * kw, kw)], piece(2, k, h), peer(2)))

    def send_x(k):
        ks = pl.ds(k * kw, kw)
        c_xh.append(send(tok_h.at[:, ks], tok.at[1, :, ks], peer(1)))

    def send_b(j):
        k, h = quads[NB + j]
        c_b.append(send(tok_h.at[pl.ds(h * hr, hr), pl.ds(k * kw, kw)], rb.at[j], peer(6)))

    def relay_b(j):
        k, h = quads[NB + j]
        c_b[j].got()
        c_z2b.append(send(rb.at[j], piece(3, k, h), peer(2)))

    def relay(i):
        k, h = quads[i]
        c_z1[i].got()
        c_z2.append(send(piece(2, k, h), piece(3, k, h), peer(6)))

    def own_fwd():
        l_blk[0].wait()

        def step(c, _):
            pre[:, col(c)] = mm(tok[0], blk[0, :, col(c)])
            return 0

        lax.fori_loop(0, NC, step, 0, unroll=True)
        tok_t[...] = tok[0].astype(F32).T.astype(BF)

    def low_fwd():
        low_t[...] = low[...].astype(F32).T.astype(BF)

    st = {}

    def run(name, *a):
        with jax.named_scope(name + "".join("_%d" % i for i in a)):
            OPS[name](*a)

    def start():
        l_tok.wait()
        l_lf.wait()
        lowf[...] = mm(tok[0], lf[...])
        lowp[...] = lowf[...].astype(BF)

    def barrier():
        pl.semaphore_wait(bar, len(peers))

    def low_rs_send():
        st["low"] = scatter(lowp, low_rs)

    def low_ag_send():
        st["low"].got()
        low[pl.ds(t * part, part), :] = gather_sum(lowf, low_rs)
        st["low_ag"] = gather(low)

    def w_low():
        l_rf.wait()
        st["low_ag"].got()

    def w_blk(i):
        l_blk[i].wait()

    def w_z1(i):
        c_z1[i].got()

    def w_xh(k):
        c_xh[k].got()

    def w_z2(k):
        for i in range(NH * k, NH * k + NH):
            (c_z2[i] if i < NB else c_z2b[i - NB]).got()

    def gelu(c):
        if c == 0:
            l_up.wait()
        cs = pl.ds(c * gw, gw)
        last = pl.ds((NK - 1) * kw, kw)
        v = pre[:, cs] + mm(tok[3, :, last], blk[3, last, cs]) + mm(low[...], rf[:, cs])
        u = up[:, cs].astype(F32)
        v2 = v * v
        th = jnp.tanh(v * (C0 + (C0 * C1) * v2))
        g = 0.5 + 0.5 * th
        act[:, cs] = (v * g).astype(BF)
        slope = g + 0.5 * v * (1.0 - th * th) * (C0 + (3.0 * C0 * C1) * v2)
        slo[:, cs] = (u * slope).astype(BF)
        n = NC // NG
        for i in range(c * n, c * n + n):
            rp[i] = mm(low_t[...], slo[:, pl.ds(i * cw, cw)]).astype(BF)
        m = mm_t(slo[:, cs], rf[:, cs])
        if c == 0:
            mixf[...] = m
        else:
            mixf[...] += m
        for i in range(c * n, c * n + n):
            r_pair(i)

    def mix_send():
        mixp[...] = mixf[...].astype(BF)
        st["mix"] = scatter(mixp, mix_rs)

    def mix_ag_send():
        st["mix"].got()
        mix[pl.ds(t * part, part), :] = gather_sum(mixf, mix_rs)
        st["mix_ag"] = gather(mix)

    half, q, e = rank // 2, rank // 8, rank // 16
    g = {}
    up_y, dn_y = dev(xl, yat(1), core), dev(xl, yat(3), core)

    def rgc(c, at, n):
        return rg.at[pl.ds(at, n), pl.ds(c * cw, cw)]

    def rq(c, k, h):
        return pl.ds(yat(k) * q + h * e, e)

    def r_pair(c):
        g["p", c] = send(rp.at[c, pl.ds((1 - core) * half, half)], rpair.at[c], pair)

    def r_s2(c):
        g["p", c].got()
        rps[c] = (rp[c, pl.ds(core * half, half)].astype(F32) + rpair[c].astype(F32)).astype(BF)
        g["yr", c] = Group([(rps.at[c, rq(c, 2, 0)], yrl.at[c, 0], up_y), (rps.at[c, rq(c, 2, 1)], yrl.at[c, 1], dn_y)], yrl.at[c])
        g["yf", c] = Group([(rps.at[c, rq(c, 1, 1)], yfin.at[c, 1], up_y), (rps.at[c, rq(c, 3, 0)], yfin.at[c, 0], dn_y)], yfin.at[c])

    def r_s2b(c):
        g["yr", c].got()
        ybs[c, 0] = (rps[c, rq(c, 1, 0)].astype(F32) + yrl[c, 0].astype(F32)).astype(BF)
        ybs[c, 1] = (rps[c, rq(c, 3, 1)].astype(F32) + yrl[c, 1].astype(F32)).astype(BF)
        g["yb", c] = Group([(ybs.at[c, 0], yb.at[c, 0], up_y), (ybs.at[c, 1], yb.at[c, 1], dn_y)], yb.at[c])

    def r_s3(c):
        g["yf", c].got()
        g["yb", c].got()
        for h in range(2):
            total = rps[c, rq(c, 0, h)].astype(F32) + yfin[c, h].astype(F32) + yb[c, h].astype(F32)
            rys[c, pl.ds(h * e, e)] = total.astype(BF)
        g["s3", c] = send(rys.at[c], rxr.at[c], xpeer)

    def r_a2(c):
        g["s3", c].got()
        at = core * half + y * q
        rg[pl.ds(at, q), pl.ds(c * cw, cw)] = ((rys[c].astype(F32) + rxr[c].astype(F32)) * scale).astype(BF)
        here = rgc(c, at, q)
        g["a2", c] = Group([(here, here, up_y), (here, here, dn_y)], rps.at[c, pl.ds(0, 2 * q)])

    def r_a2b(c):
        g["a2", c].got()
        one = rgc(c, core * half + yat(3) * q, e)
        two = rgc(c, core * half + yat(1) * q + e, e)
        g["a2b", c] = Group([(one, one, up_y), (two, two, dn_y)], yb.at[c])

    def r_a3(c):
        g["a2b", c].got()
        here = rgc(c, core * half, half)
        g["a3", c] = send(here, here, pair)

    def r_end(c):
        g["a3", c].got()

    def gcol(ref, i, k, n=NK):
        w = db // n
        return ref.at[i, :, pl.ds(k * w, w)]

    NX = 6

    def p2(k):
        ks = pl.ds(k * kw, kw)
        gs[0, :, ks] = mm_t(slo[...], blk[3, ks, :]).astype(BF)

    def p2_send(k):
        g["g2", k] = send(gcol(gs, 0, k, NX), gcol(gr, 0, k, NX), peer(6))

    def px(k):
        ks = pl.ds(k * kw, kw)
        gs[1, :, ks] = mm_t(slo[...], blk[1, ks, :]).astype(BF)

    def px_send(k):
        g["gx", k] = send(gcol(gs, 1, k, NX), gcol(gr, 1, k, NX), peer(1))

    def p1(k):
        ks = pl.ds(k * kw, kw)
        pre[:, ks] = mm_t(slo[...], blk[2, ks, :])

    def p1_send(k):
        ks = pl.ds(k * kw, kw)
        g["g2", 2 * k].got()
        g["g2", 2 * k + 1].got()
        gs[2, :, ks] = (pre[:, ks] + gr[0, :, ks].astype(F32)).astype(BF)
        g["g1", k] = send(gcol(gs, 2, k), gcol(gr, 2, k), peer(2))

    def p0(k):
        ks = pl.ds(k * kw, kw)
        own[:, ks] = mm_t(slo[...], blk[0, ks, :])

    lh, le = db // 2, db // 16

    def left():
        st["mix_ag"].got()
        lp[...] = mm(tok_t[...], mix[...]).astype(BF)
        g["lp"] = send(lp.at[pl.ds((1 - core) * lh, lh)], lpair, pair)

    def tg_low():
        own[...] += mm_t(mix[...], lf[...])

    def left_rs():
        g["lp"].got()
        lps[...] = (lp[pl.ds(core * lh, lh)].astype(F32) + lpair[...].astype(F32)).astype(BF)
        cs = []
        for i, (k, f) in enumerate(chips):
            xx = xl if f == 0 else 1 - xl
            cs.append((lps.at[pl.ds(yat(k) * (2 * le) + xx * le, le)], l7r.at[i], chip(k, f)))
        g["l7"] = Group(cs, l7r)

    def left_ag():
        g["l7"].got()
        at = y * (2 * le) + xl * le
        total = lps[pl.ds(at, le)].astype(F32)
        for i in range(7):
            total = total + l7r[i].astype(F32)
        lg[pl.ds(core * lh + at, le)] = (total * scale).astype(BF)
        here = lg.at[pl.ds(core * lh + at, le)]
        g["la"] = Group([(here, here, chip(k, f)) for k, f in chips], l7r)

    def left_pair():
        g["la"].got()
        here = lg.at[pl.ds(core * lh, lh)]
        g["lap"] = send(here, here, pair)

    def left_end():
        g["lap"].got()

    def tg_end():
        for k in range(NX):
            g["gx", k].got()
        for k in range(NK):
            g["g1", k].got()
        tg[...] = (own[...] + gr[1].astype(F32) + gr[2].astype(F32)).astype(BF)

    def finish():
        for c in groups:
            c.sent()

    OPS = dict(locals())
    for name, *a in ORDER:
        run(name, *a)


ORDER = [
    ("start",), ("barrier",), ("send_z", 0), ("send_b", 0), ("low_rs_send",), ("send_z", 1), ("send_x", 0), ("send_b", 1),
    *[("send_z", i) for i in range(2, 8)], ("send_x", 1), *[("send_z", i) for i in range(8, 12)], ("send_x", 2), ("own_fwd",),
    ("relay", 0), ("relay_b", 0), ("relay", 1), ("relay", 2), ("relay_b", 1), ("low_ag_send",), ("relay", 3), ("w_blk", 1), ("w_blk", 2),
    ("add_k", 2, 0), ("relay", 4), ("relay", 5), ("w_xh", 0), ("add_k", 1, 0), ("relay", 6), ("relay", 7),
    ("add_k", 2, 1), ("relay", 8), ("relay", 9), ("w_xh", 1), ("add_k", 1, 1), ("w_z1", 10), ("w_z1", 11),
    ("add_k", 2, 2), ("w_blk", 3), ("w_z2", 0), ("add_k", 3, 0), ("w_xh", 2), ("add_k", 1, 2),
    ("w_z2", 1), ("add_k", 3, 1), ("w_low",), ("low_fwd",), ("w_z2", 2),
    ("gelu", 0), ("gelu", 1), ("r_s2", 0), ("r_s2", 1), ("gelu", 2), ("mix_send",), ("r_s2", 2), ("r_s2", 3),
    ("px", 0), ("px_send", 0), ("px_send", 1), ("r_s2", 4), ("r_s2", 5), ("r_s2b", 0), ("r_s2b", 1), ("px", 1), ("r_s2b", 2), ("r_s2b", 3),
    ("px", 2), ("mix_ag_send",), ("r_s2b", 4), ("r_s2b", 5), ("r_s3", 0), ("r_s3", 1), ("px_send", 2), ("p2", 0), ("p2_send", 0), ("p2_send", 1),
    ("r_s3", 2), ("r_s3", 3), ("p2", 1), ("p2_send", 2), ("p2_send", 3), ("r_s3", 4), ("r_s3", 5), ("r_a2", 0), ("left",), ("r_a2", 1), ("p2", 2), ("p2_send", 4), ("p2_send", 5),
    ("px_send", 3), ("left_rs",), ("r_a2", 2), ("r_a2", 3), ("r_a2b", 0), ("p1", 0), ("p1_send", 0), ("px_send", 4), ("r_a2", 4), ("r_a2b", 1), ("r_a2", 5),
    ("p1", 1), ("p1_send", 1), ("px_send", 5), ("p1", 2), ("p1_send", 2), ("r_a2b", 2), ("p0", 0), ("r_a2b", 3), ("r_a3", 0), ("left_ag",), ("p0", 1), ("r_a2b", 4), ("r_a3", 1), ("r_a2b", 5), ("p0", 2), ("r_a3", 2),
    ("r_a3", 3), ("tg_low",), ("r_a3", 4), ("left_pair",), ("r_a3", 5), ("tg_end",),
    *[("r_end", i) for i in range(6)], ("left_end",), ("finish",),
]
NB = 10
NH = 4
N_SEND = 20
N_RECV = 100


def move(*refs):
    n = len(refs) // 2
    sem = refs[-1]
    cs = []
    for i in range(n):
        rows = refs[i].shape[0] // CUTS[i]
        for k in range(CUTS[i]):
            at = pl.ds(k * rows, rows)
            cs.append(pltpu.make_async_copy(refs[i].at[at], refs[n + i].at[at], sem.at[len(cs)]))
    for c in cs:
        c.start()
    for c in cs:
        c.wait()


CUTS = (4, 1, 1, 4)


def body(scale, tokens, blocks, left_factor, right_factor, upstream):
    rows, db = tokens.shape
    ns, _, fb = blocks.shape
    rank = left_factor.shape[1]
    cw = fb // NC
    part = rows // 8
    shapes = [
        jax.ShapeDtypeStruct((rows, fb), BF),
        jax.ShapeDtypeStruct((rows, db), BF),
        jax.ShapeDtypeStruct((db, rank), BF),
        jax.ShapeDtypeStruct((rank, fb), BF),
    ]
    V = pltpu.VMEM
    scratch = [
        V((ns, db, fb), BF), V((ns, rows, db), BF), V((db, rows), BF), V((db, rank), BF),
        V((rank, fb), BF), V((rows, fb), BF), V((rows, fb), F32), V((rows, fb), BF),
        V((rows, rank), F32), V((rows, rank), BF), V((7, part, rank), BF), V((rows, rank), BF), V((rank, rows), BF),
        V((rows, rank), F32), V((rows, rank), BF), V((7, part, rank), BF), V((rows, rank), BF),
        V((2, rows // NH, db // NK), BF), V((3, rows, db), BF), V((3, rows, db), BF), V((rows, db), F32),
        V((NC, rank, cw), BF), V((NC, rank // 2, cw), BF), V((NC, rank // 2, cw), BF),
        *[V((NC, 2, rank // 16, cw), BF)] * 4, V((NC, rank // 8, cw), BF), V((NC, rank // 8, cw), BF),
        V((db, rank), BF), V((db // 2, rank), BF), V((db // 2, rank), BF), V((7, db // 16, rank), BF),
        pltpu.SemaphoreType.DMA((8,)), pltpu.SemaphoreType.DMA((N_SEND,)), pltpu.SemaphoreType.DMA((N_RECV,)),
    ]
    any_spec = pl.BlockSpec(memory_space=pl.ANY)
    vmem_spec = pl.BlockSpec(memory_space=pltpu.VMEM)
    res = pl.pallas_call(
        functools.partial(kernel, scale, (rows, db, fb, rank)),
        out_shape=[V(o.shape, o.dtype) for o in shapes],
        in_specs=[any_spec] * 5,
        out_specs=[vmem_spec] * 4,
        scratch_shapes=scratch,
        compiler_params=pltpu.CompilerParams(
            collective_id=0, has_side_effects=True, vmem_limit_bytes=56 * 1024 * 1024
        ),
    )(tokens, blocks, left_factor, right_factor, upstream)
    return pl.pallas_call(
        move,
        out_shape=shapes,
        in_specs=[vmem_spec] * 4,
        out_specs=[any_spec] * 4,
        scratch_shapes=[pltpu.SemaphoreType.DMA((sum(CUTS),))],
        compiler_params=pltpu.CompilerParams(vmem_limit_bytes=1024 * 1024),
    )(*[pltpu.with_memory_space_constraint(r, pltpu.VMEM) for r in res])


def solution(mesh):
    placed = (
        P("dp", "tensor"),
        P(None, "tensor", None),
        P("tensor", None),
        P(None, "tensor"),
        P("dp", "tensor"),
    )

    def whole(tokens, blocks, left_factor, right_factor, upstream):
        scale = 1.0 / float(tokens.shape[0]) ** 0.5
        return jax.shard_map(
            functools.partial(body, scale),
            mesh=mesh,
            in_specs=placed,
            out_specs=(P("dp", "tensor"), P("dp", "tensor"), P("tensor", None), P(None, "tensor")),
            check_vma=False,
        )(tokens, blocks, left_factor, right_factor, upstream)

    return whole
```

```python
import functools

import jax
import jax.numpy as jnp
from jax import lax
from jax.experimental import pallas as pl
from jax.experimental.pallas import tpu as pltpu
from jax.sharding import PartitionSpec as P

MESH = pl.DeviceIdType.MESH
BF = jnp.bfloat16
F32 = jnp.float32
C0 = 0.7978845608028654
C1 = 0.044715

NC = 6
NG = 3
NK = 3


def flip(v, mask):
    for b in range(3):
        if mask >> b & 1:
            bit = lax.rem(lax.div(v, 1 << b), 2)
            v = v + (1 - 2 * bit) * (1 << b)
    return v


def mm(a, b):
    return jnp.dot(a, b, preferred_element_type=F32)


def mm_t(a, b):
    return lax.dot_general(a, b, (((1,), (1,)), ((), ())), preferred_element_type=F32)


def kernel(scale, sizes, tok_h, blk_h, lf_h, rf_h, up_h, act, tg, lg, rg,
           blk, tok, tok_t, lf, rf, up, pre, slo,
           lowf, lowp, low_rs, low, low_t,
           mixf, mixp, mix_rs, mix,
           rb, gs, gr, own,
           rp, rpair, rps, yrl, yfin, ybs, yb, rys, rxr,
           lp, lpair, lps, l7r,
           load_sem, send_sem, recv_sem):
    rows, db, fb, rank = sizes
    cw, kw, gw = fb // NC, db // NK, fb // NG
    part = rows // 8
    d = lax.axis_index("dp")
    t = lax.axis_index("tensor")
    core = lax.rem(d, 2)
    y = lax.rem(lax.div(d, 2), 4)
    xl = lax.div(d, 8)

    def dev(x, yy, c):
        return (x * 8 + yy * 2 + c, t)

    def peer(mask):
        return (d, flip(t, mask))

    def yat(k):
        return lax.rem(y + k, 4)

    pair = dev(xl, y, 1 - core)
    xpeer = dev(1 - xl, y, core)
    chips = [(k, f) for f in range(2) for k in (2, 1, 3, 0) if (k, f) != (0, 0)]

    def chip(k, f):
        return dev(xl if f == 0 else 1 - xl, yat(k), core)

    bar = pltpu.get_barrier_semaphore()
    peers = [peer(m) for m in (7, 5, 6, 4, 3, 1, 2)] + [chip(k, f) for k, f in chips] + [pair]
    for p in peers:
        pl.semaphore_signal(bar, inc=1, device_id=p, device_id_type=MESH)

    loads = []

    def load(src, dst):
        c = pltpu.make_async_copy(src, dst, load_sem.at[len(loads)])
        c.start()
        loads.append(c)
        return c

    l_tok = load(tok_h, tok.at[0])
    l_lf = load(lf_h, lf)
    l_blk = {}
    for i in (0, 2, 1, 3):
        l_blk[i] = load(blk_h.at[i], blk.at[i])
    l_rf = load(rf_h, rf)
    l_up = load(up_h, up)

    groups, slots = [], {}

    class Group:
        def __init__(self, copies, size, key=None):
            n = len(groups)
            if n >= N_SEND:
                groups[n - N_SEND].sent()
            m = slots.setdefault(n if key is None else key, len(slots))
            self.ssem, self.rsem, self.size, self.open = send_sem.at[n % N_SEND], recv_sem.at[m], size, True
            groups.append(self)
            for src, dst, to in copies:
                pltpu.make_async_remote_copy(
                    src_ref=src, dst_ref=dst, send_sem=self.ssem, recv_sem=self.rsem,
                    device_id=to, device_id_type=MESH).start()

        def got(self, size=None):
            size = self.size if size is None else size
            pltpu.make_async_copy(size, size, self.rsem).wait()

        def sent(self):
            if self.open:
                pltpu.make_async_copy(self.size, self.size, self.ssem).wait()
                self.open = False

    def send(src, dst, to, key=None):
        return Group([(src, dst, to)], dst, key)

    def scatter(src, dst):
        return Group([(src.at[pl.ds(flip(t, m) * part, part)], dst.at[m - 1], peer(m)) for m in (7, 5, 6, 4, 3, 1, 2)], dst)

    def gather(buf):
        here = buf.at[pl.ds(t * part, part)]
        return Group([(here, here, peer(m)) for m in (7, 5, 6, 4, 3, 1, 2)], buf.at[pl.ds(0, 7 * part)])

    def gather_sum(f32_ref, recv):
        total = f32_ref[pl.ds(t * part, part), :]
        for m in range(7):
            total = total + recv[m].astype(F32)
        return total.astype(BF)

    def col(c):
        return pl.ds(pl.multiple_of(c * cw, cw), cw)

    def add_k(s, k):
        ks = pl.ds(k * kw, kw)

        def step(c, _):
            pre[:, col(c)] += mm(tok[s, :, ks], blk[s, ks, col(c)])
            return 0

        lax.fori_loop(0, NC, step, 0, unroll=True)

    hr = rows // NH
    quads = [(k, h) for k in range(NK) for h in range(NH)]

    def piece(s, k, h):
        return tok.at[s, pl.ds(h * hr, hr), pl.ds(k * kw, kw)]

    c_z1, c_xh, c_z2, c_b, c_z2b = [], [], [], [], []

    def send_z(i):
        k, h = quads[i]
        c_z1.append(send(tok_h.at[pl.ds(h * hr, hr), pl.ds(k * kw, kw)], piece(2, k, h), peer(2)))

    def send_x(k):
        ks = pl.ds(k * kw, kw)
        c_xh.append(send(tok_h.at[:, ks], tok.at[1, :, ks], peer(1)))

    def send_b(j):
        k, h = quads[NB + j]
        c_b.append(send(tok_h.at[pl.ds(h * hr, hr), pl.ds(k * kw, kw)], rb.at[j], peer(6)))

    def relay_b(j):
        k, h = quads[NB + j]
        c_b[j].got()
        c_z2b.append(send(rb.at[j], piece(3, k, h), peer(2), "z2_%d" % k))

    def relay(i):
        k, h = quads[i]
        c_z1[i].got()
        c_z2.append(send(piece(2, k, h), piece(3, k, h), peer(6), "z2_%d" % k))

    def own_fwd():
        l_blk[0].wait()

        def step(c, _):
            pre[:, col(c)] = mm(tok[0], blk[0, :, col(c)])
            return 0

        lax.fori_loop(0, NC, step, 0, unroll=True)
        tok_t[...] = tok[0].astype(F32).T.astype(BF)

    def low_fwd():
        low_t[...] = low[...].astype(F32).T.astype(BF)

    st = {}

    def run(name, *a):
        with jax.named_scope(name + "".join("_%d" % i for i in a)):
            OPS[name](*a)

    def start():
        l_tok.wait()
        l_lf.wait()
        lowf[...] = mm(tok[0], lf[...])
        lowp[...] = lowf[...].astype(BF)

    def barrier():
        pl.semaphore_wait(bar, len(peers))

    def low_rs_send():
        st["low"] = scatter(lowp, low_rs)

    def low_ag_send():
        st["low"].got()
        low[pl.ds(t * part, part), :] = gather_sum(lowf, low_rs)
        st["low_ag"] = gather(low)

    def w_low():
        l_rf.wait()
        st["low_ag"].got()

    def w_blk(i):
        l_blk[i].wait()

    def w_z1(i):
        c_z1[i].got()

    def w_xh(k):
        c_xh[k].got()

    def w_z2(k):
        c_z2[NH * k].got(tok.at[3, :, pl.ds(k * kw, kw)])

    def gelu(c):
        if c == 0:
            l_up.wait()
        cs = pl.ds(c * gw, gw)
        last = pl.ds((NK - 1) * kw, kw)
        v = pre[:, cs] + mm(jnp.concatenate([tok[3, :, last], low[...]], 1), jnp.concatenate([blk[3, last, cs], rf[:, cs]], 0))
        u = up[:, cs].astype(F32)
        v2 = v * v
        th = jnp.tanh(v * (C0 + (C0 * C1) * v2))
        g = 0.5 + 0.5 * th
        act[:, cs] = (v * g).astype(BF)
        slope = g + 0.5 * v * (1.0 - th * th) * (C0 + (3.0 * C0 * C1) * v2)
        slo[:, cs] = (u * slope).astype(BF)
        n = NC // NG
        for i in range(c * n, c * n + n):
            rp[i] = mm(low_t[...], slo[:, pl.ds(i * cw, cw)]).astype(BF)
        m = mm_t(slo[:, cs], rf[:, cs])
        if c == 0:
            mixf[...] = m
        else:
            mixf[...] += m
        for i in range(c * n, c * n + n):
            r_pair(i)

    def mix_send():
        mixp[...] = mixf[...].astype(BF)
        st["mix"] = scatter(mixp, mix_rs)

    def mix_ag_send():
        st["mix"].got()
        mix[pl.ds(t * part, part), :] = gather_sum(mixf, mix_rs)
        st["mix_ag"] = gather(mix)

    half, q, e = rank // 2, rank // 8, rank // 16
    g = {}
    up_y, dn_y = dev(xl, yat(1), core), dev(xl, yat(3), core)

    def rgc(c, at, n):
        return rg.at[pl.ds(at, n), pl.ds(c * cw, cw)]

    def rq(c, k, h):
        return pl.ds(yat(k) * q + h * e, e)

    def r_pair(c):
        g["p", c] = send(rp.at[c, pl.ds((1 - core) * half, half)], rpair.at[c], pair)

    def r_s2(c):
        g["p", c].got()
        rps[c] = (rp[c, pl.ds(core * half, half)].astype(F32) + rpair[c].astype(F32)).astype(BF)
        g["yr", c] = Group([(rps.at[c, rq(c, 2, 0)], yrl.at[c, 0], up_y), (rps.at[c, rq(c, 2, 1)], yrl.at[c, 1], dn_y)], yrl.at[c])
        g["yf", c] = Group([(rps.at[c, rq(c, 1, 1)], yfin.at[c, 1], up_y), (rps.at[c, rq(c, 3, 0)], yfin.at[c, 0], dn_y)], yfin.at[c], "y_%d" % c)

    def r_s2b(c):
        g["yr", c].got()
        ybs[c, 0] = (rps[c, rq(c, 1, 0)].astype(F32) + yrl[c, 0].astype(F32)).astype(BF)
        ybs[c, 1] = (rps[c, rq(c, 3, 1)].astype(F32) + yrl[c, 1].astype(F32)).astype(BF)
        g["yb", c] = Group([(ybs.at[c, 0], yb.at[c, 0], up_y), (ybs.at[c, 1], yb.at[c, 1], dn_y)], yb.at[c], "y_%d" % c)

    def r_s3(c):
        g["yf", c].got(rps.at[c, pl.ds(0, 4 * e)])
        for h in range(2):
            total = rps[c, rq(c, 0, h)].astype(F32) + yfin[c, h].astype(F32) + yb[c, h].astype(F32)
            rys[c, pl.ds(h * e, e)] = total.astype(BF)
        g["s3", c] = send(rys.at[c], rxr.at[c], xpeer)

    def r_a2(c):
        g["s3", c].got()
        at = core * half + y * q
        rg[pl.ds(at, q), pl.ds(c * cw, cw)] = ((rys[c].astype(F32) + rxr[c].astype(F32)) * scale).astype(BF)
        here = rgc(c, at, q)
        g["a2", c] = Group([(here, here, up_y), (here, here, dn_y)], rps.at[c, pl.ds(0, 2 * q)])

    def r_a2b(c):
        g["a2", c].got()
        one = rgc(c, core * half + yat(3) * q, e)
        two = rgc(c, core * half + yat(1) * q + e, e)
        g["a2b", c] = Group([(one, one, up_y), (two, two, dn_y)], yb.at[c])

    def r_a3(c):
        g["a2b", c].got()
        here = rgc(c, core * half, half)
        g["a3", c] = send(here, here, pair, "a3")

    def r_end():
        g["a3", 0].got(rg.at[pl.ds(0, half)])

    def gcol(ref, i, k, n=NK):
        w = db // n
        return ref.at[i, :, pl.ds(k * w, w)]

    NX = 6

    def p2(k):
        ks = pl.ds(k * (db // 2), db // 2)
        gs[0, :, ks] = mm_t(slo[...], blk[3, ks, :]).astype(BF)

    def p2_send(k):
        g["g2", k] = send(gcol(gs, 0, k, NX), gcol(gr, 0, k, NX), peer(6), "g2_%d" % (k // 2))

    def px(k):
        ks = pl.ds(k * (db // 2), db // 2)
        gs[1, :, ks] = mm_t(slo[...], blk[1, ks, :]).astype(BF)

    def px_send(k):
        g["gx", k] = send(gcol(gs, 1, k, NX), gcol(gr, 1, k, NX), peer(1), "gx")

    def p1(k):
        ks = pl.ds(k * (db // 2), db // 2)
        pre[:, ks] = mm_t(slo[...], blk[2, ks, :])

    def p1_send(k):
        ks = pl.ds(k * kw, kw)
        g["g2", 2 * k].got(gcol(gr, 0, k))
        gs[2, :, ks] = (pre[:, ks] + gr[0, :, ks].astype(F32)).astype(BF)
        g["g1", k] = send(gcol(gs, 2, k), gcol(gr, 2, k), peer(2), "g1")

    def p0(k):
        ks = pl.ds(k * (db // 2), db // 2)
        own[:, ks] = mm_t(slo[...], blk[0, ks, :])

    lh, le = db // 2, db // 16

    def left():
        st["mix_ag"].got()
        lp[...] = mm(tok_t[...], mix[...]).astype(BF)
        g["lp"] = send(lp.at[pl.ds((1 - core) * lh, lh)], lpair, pair)

    def tg_low():
        own[...] += mm_t(mix[...], lf[...])

    def left_rs():
        g["lp"].got()
        lps[...] = (lp[pl.ds(core * lh, lh)].astype(F32) + lpair[...].astype(F32)).astype(BF)
        cs = []
        for i, (k, f) in enumerate(chips):
            xx = xl if f == 0 else 1 - xl
            cs.append((lps.at[pl.ds(yat(k) * (2 * le) + xx * le, le)], l7r.at[i], chip(k, f)))
        g["l7"] = Group(cs, l7r)

    def left_ag():
        g["l7"].got()
        at = y * (2 * le) + xl * le
        total = lps[pl.ds(at, le)].astype(F32)
        for i in range(7):
            total = total + l7r[i].astype(F32)
        lg[pl.ds(core * lh + at, le)] = (total * scale).astype(BF)
        here = lg.at[pl.ds(core * lh + at, le)]
        g["la"] = Group([(here, here, chip(k, f)) for k, f in chips], l7r)

    def left_pair():
        g["la"].got()
        here = lg.at[pl.ds(core * lh, lh)]
        g["lap"] = send(here, here, pair)

    def left_end():
        g["lap"].got()

    def tg_end():
        g["gx", 0].got(gr.at[1])
        g["g1", 0].got(gr.at[2])
        tg[...] = (own[...] + gr[1].astype(F32) + gr[2].astype(F32)).astype(BF)

    def finish():
        for c in groups:
            c.sent()

    OPS = dict(locals())
    for name, *a in ORDER:
        run(name, *a)
    assert len(slots) == N_RECV


ORDER = [
    ("start",), ("barrier",), ("send_z", 0), ("send_b", 0), ("low_rs_send",), ("send_z", 1), ("send_x", 0), ("send_b", 1),
    *[("send_z", i) for i in range(2, 8)], ("send_x", 1), *[("send_z", i) for i in range(8, 12)], ("send_x", 2), ("own_fwd",),
    ("relay", 0), ("relay_b", 0), ("relay", 1), ("low_ag_send",), ("relay", 2), ("relay_b", 1), ("relay", 3), ("w_blk", 1), ("w_blk", 2),
    ("add_k", 2, 0), ("relay", 4), ("relay", 5), ("w_xh", 0), ("add_k", 1, 0), ("relay", 6), ("relay", 7),
    ("add_k", 2, 1), ("relay", 8), ("relay", 9), ("w_xh", 1), ("add_k", 1, 1), ("w_z1", 10), ("w_z1", 11),
    ("add_k", 2, 2), ("w_blk", 3), ("w_z2", 0), ("add_k", 3, 0), ("w_xh", 2), ("add_k", 1, 2),
    ("w_z2", 1), ("add_k", 3, 1), ("w_low",), ("low_fwd",), ("w_z2", 2),
    ("gelu", 0), ("gelu", 1), ("r_s2", 0), ("r_s2", 1), ("gelu", 2), ("mix_send",), ("r_s2", 2), ("r_s2", 3),
    ("px", 0), ("px_send", 0), ("px_send", 1), ("r_s2", 4), ("r_s2", 5), ("r_s2b", 0), ("r_s2b", 1), ("px", 1), ("r_s2b", 2), ("r_s2b", 3),
    ("p2", 0), ("mix_ag_send",), ("p2_send", 0), ("p2_send", 1), ("r_s2b", 4), ("r_s2b", 5), ("r_s3", 0), ("r_s3", 1), ("px_send", 2), ("p2", 1), ("p2_send", 2),
    ("r_s3", 2), ("r_s3", 3), ("p2_send", 3), ("r_s3", 4), ("r_s3", 5), ("p1", 0), ("r_a2", 0), ("p2_send", 4), ("left",), ("p2_send", 5), ("r_a2", 1),
    ("px_send", 3), ("p1", 1), ("left_rs",), ("r_a2", 2), ("r_a2", 3), ("r_a2b", 0), ("p1_send", 0), ("px_send", 4), ("r_a2", 4), ("r_a2b", 1), ("r_a2", 5), ("p1_send", 1),
    ("px_send", 5), ("p0", 0), ("p1_send", 2), ("r_a2b", 2), ("p0", 1), ("r_a2b", 3), ("r_a3", 0), ("left_ag",), ("tg_low",), ("r_a2b", 4), ("r_a3", 1), ("r_a2b", 5), ("r_a3", 2),
    ("r_a3", 3), ("r_a3", 4), ("left_pair",), ("r_a3", 5), ("tg_end",), ("r_end",), ("left_end",), ("finish",),
]
NB = 10
NH = 4
N_SEND = 20
N_RECV = 70


def move(*refs):
    n = len(refs) // 2
    sem = refs[-1]
    cs = []
    for i in range(n):
        rows = refs[i].shape[0] // CUTS[i]
        for k in range(CUTS[i]):
            at = pl.ds(k * rows, rows)
            cs.append(pltpu.make_async_copy(refs[i].at[at], refs[n + i].at[at], sem.at[len(cs)]))
    for c in cs:
        c.start()
    for c in cs:
        c.wait()


CUTS = (4, 1, 1, 4)


def body(scale, tokens, blocks, left_factor, right_factor, upstream):
    rows, db = tokens.shape
    ns, _, fb = blocks.shape
    rank = left_factor.shape[1]
    cw = fb // NC
    part = rows // 8
    shapes = [
        jax.ShapeDtypeStruct((rows, fb), BF),
        jax.ShapeDtypeStruct((rows, db), BF),
        jax.ShapeDtypeStruct((db, rank), BF),
        jax.ShapeDtypeStruct((rank, fb), BF),
    ]
    V = pltpu.VMEM
    scratch = [
        V((ns, db, fb), BF), V((ns, rows, db), BF), V((db, rows), BF), V((db, rank), BF),
        V((rank, fb), BF), V((rows, fb), BF), V((rows, fb), F32), V((rows, fb), BF),
        V((rows, rank), F32), V((rows, rank), BF), V((7, part, rank), BF), V((rows, rank), BF), V((rank, rows), BF),
        V((rows, rank), F32), V((rows, rank), BF), V((7, part, rank), BF), V((rows, rank), BF),
        V((2, rows // NH, db // NK), BF), V((3, rows, db), BF), V((3, rows, db), BF), V((rows, db), F32),
        V((NC, rank, cw), BF), V((NC, rank // 2, cw), BF), V((NC, rank // 2, cw), BF),
        *[V((NC, 2, rank // 16, cw), BF)] * 4, V((NC, rank // 8, cw), BF), V((NC, rank // 8, cw), BF),
        V((db, rank), BF), V((db // 2, rank), BF), V((db // 2, rank), BF), V((7, db // 16, rank), BF),
        pltpu.SemaphoreType.DMA((8,)), pltpu.SemaphoreType.DMA((N_SEND,)), pltpu.SemaphoreType.DMA((N_RECV,)),
    ]
    any_spec = pl.BlockSpec(memory_space=pl.ANY)
    vmem_spec = pl.BlockSpec(memory_space=pltpu.VMEM)
    res = pl.pallas_call(
        functools.partial(kernel, scale, (rows, db, fb, rank)),
        out_shape=[V(o.shape, o.dtype) for o in shapes],
        in_specs=[any_spec] * 5,
        out_specs=[vmem_spec] * 4,
        scratch_shapes=scratch,
        compiler_params=pltpu.CompilerParams(
            collective_id=0, has_side_effects=True, vmem_limit_bytes=56 * 1024 * 1024
        ),
    )(tokens, blocks, left_factor, right_factor, upstream)
    return pl.pallas_call(
        move,
        out_shape=shapes,
        in_specs=[vmem_spec] * 4,
        out_specs=[any_spec] * 4,
        scratch_shapes=[pltpu.SemaphoreType.DMA((sum(CUTS),))],
        compiler_params=pltpu.CompilerParams(vmem_limit_bytes=1024 * 1024),
    )(*[pltpu.with_memory_space_constraint(r, pltpu.VMEM) for r in res])


def solution(mesh):
    placed = (
        P("dp", "tensor"),
        P(None, "tensor", None),
        P("tensor", None),
        P(None, "tensor"),
        P("dp", "tensor"),
    )

    def whole(tokens, blocks, left_factor, right_factor, upstream):
        scale = 1.0 / float(tokens.shape[0]) ** 0.5
        return jax.shard_map(
            functools.partial(body, scale),
            mesh=mesh,
            in_specs=placed,
            out_specs=(P("dp", "tensor"), P("dp", "tensor"), P("tensor", None), P(None, "tensor")),
            check_vma=False,
        )(tokens, blocks, left_factor, right_factor, upstream)

    return whole
```

```python
import functools

import jax
import jax.numpy as jnp
from jax import lax
from jax.experimental import pallas as pl
from jax.experimental.pallas import tpu as pltpu
from jax.sharding import PartitionSpec as P

MESH = pl.DeviceIdType.MESH
BF = jnp.bfloat16
F32 = jnp.float32
C0 = 0.7978845608028654
C1 = 0.044715

NC = 6
NG = 3
NK = 3


def flip(v, mask):
    for b in range(3):
        if mask >> b & 1:
            bit = lax.rem(lax.div(v, 1 << b), 2)
            v = v + (1 - 2 * bit) * (1 << b)
    return v


def mm(a, b):
    return jnp.dot(a, b, preferred_element_type=F32)


def mm_t(a, b):
    return lax.dot_general(a, b, (((1,), (1,)), ((), ())), preferred_element_type=F32)


def kernel(scale, sizes, tok_h, blk_h, lf_h, rf_h, up_h, act, tg, lg, rg,
           blk, tok, tok_t, lf, rf, up, pre, slo,
           lowf, lowp, low_rs, low, low_t,
           mixf, mixp, mix_rs, mix,
           rb, gs, gr, own,
           rp, rpair, rps, yrl, yfin, ybs, yb, rys, rxr,
           lp, lpair, lps, l7r,
           load_sem, send_sem, recv_sem):
    rows, db, fb, rank = sizes
    cw, kw, gw = fb // NC, db // NK, fb // NG
    part = rows // 8
    d = lax.axis_index("dp")
    t = lax.axis_index("tensor")
    core = lax.rem(d, 2)
    y = lax.rem(lax.div(d, 2), 4)
    xl = lax.div(d, 8)

    def dev(x, yy, c):
        return (x * 8 + yy * 2 + c, t)

    def peer(mask):
        return (d, flip(t, mask))

    def yat(k):
        return lax.rem(y + k, 4)

    pair = dev(xl, y, 1 - core)
    xpeer = dev(1 - xl, y, core)
    chips = [(k, f) for f in range(2) for k in (2, 1, 3, 0) if (k, f) != (0, 0)]

    def chip(k, f):
        return dev(xl if f == 0 else 1 - xl, yat(k), core)

    bar = pltpu.get_barrier_semaphore()
    peers = [peer(m) for m in (7, 5, 6, 4, 3, 1, 2)] + [chip(k, f) for k, f in chips] + [pair]
    for p in peers:
        pl.semaphore_signal(bar, inc=1, device_id=p, device_id_type=MESH)

    loads = []

    def load(src, dst):
        c = pltpu.make_async_copy(src, dst, load_sem.at[len(loads)])
        c.start()
        loads.append(c)
        return c

    l_tok = load(tok_h, tok.at[0])
    l_lf = load(lf_h, lf)
    l_blk = {}
    for i in (0, 2, 1, 3):
        l_blk[i] = load(blk_h.at[i], blk.at[i])
    l_rf = load(rf_h, rf)
    l_up = load(up_h, up)

    groups, slots = [], {}

    class Group:
        def __init__(self, copies, size, key=None):
            n = len(groups)
            if n >= N_SEND:
                groups[n - N_SEND].sent()
            m = slots.setdefault(n if key is None else key, len(slots))
            self.ssem, self.rsem, self.size, self.open = send_sem.at[n % N_SEND], recv_sem.at[m], size, True
            groups.append(self)
            for src, dst, to in copies:
                pltpu.make_async_remote_copy(
                    src_ref=src, dst_ref=dst, send_sem=self.ssem, recv_sem=self.rsem,
                    device_id=to, device_id_type=MESH).start()

        def got(self, size=None):
            size = self.size if size is None else size
            pltpu.make_async_copy(size, size, self.rsem).wait()

        def sent(self):
            if self.open:
                pltpu.make_async_copy(self.size, self.size, self.ssem).wait()
                self.open = False

    def send(src, dst, to, key=None):
        return Group([(src, dst, to)], dst, key)

    def scatter(src, dst):
        return Group([(src.at[pl.ds(flip(t, m) * part, part)], dst.at[m - 1], peer(m)) for m in (7, 5, 6, 4, 3, 1, 2)], dst)

    def gather(buf):
        here = buf.at[pl.ds(t * part, part)]
        return Group([(here, here, peer(m)) for m in (7, 5, 6, 4, 3, 1, 2)], buf.at[pl.ds(0, 7 * part)])

    def gather_sum(f32_ref, recv):
        total = f32_ref[pl.ds(t * part, part), :]
        for m in range(7):
            total = total + recv[m].astype(F32)
        return total.astype(BF)

    def col(c):
        return pl.ds(pl.multiple_of(c * cw, cw), cw)

    def add_k(s, k):
        ks = pl.ds(k * kw, kw)

        def step(c, _):
            pre[:, col(c)] += mm(tok[s, :, ks], blk[s, ks, col(c)])
            return 0

        lax.fori_loop(0, NC, step, 0, unroll=True)

    hr = rows // NH
    quads = [(k, h) for k in range(NK) for h in range(NH)]

    def piece(s, k, h):
        return tok.at[s, pl.ds(h * hr, hr), pl.ds(k * kw, kw)]

    c_z1, c_xh, c_z2, c_b, c_z2b = [], [], [], [], []

    def send_z(i):
        k, h = quads[i]
        c_z1.append(send(tok_h.at[pl.ds(h * hr, hr), pl.ds(k * kw, kw)], piece(2, k, h), peer(2)))

    def send_x(k):
        ks = pl.ds(k * kw, kw)
        c_xh.append(send(tok_h.at[:, ks], tok.at[1, :, ks], peer(1)))

    def send_b(j):
        k, h = quads[NB + j]
        c_b.append(send(tok_h.at[pl.ds(h * hr, hr), pl.ds(k * kw, kw)], rb.at[j], peer(6)))

    def relay_b(j):
        k, h = quads[NB + j]
        c_b[j].got()
        c_z2b.append(send(rb.at[j], piece(3, k, h), peer(2), "z2_%d" % k))

    def relay(i):
        k, h = quads[i]
        c_z1[i].got()
        c_z2.append(send(piece(2, k, h), piece(3, k, h), peer(6), "z2_%d" % k))

    def own_fwd():
        l_blk[0].wait()

        def step(c, _):
            pre[:, col(c)] = mm(tok[0], blk[0, :, col(c)])
            return 0

        lax.fori_loop(0, NC, step, 0, unroll=True)
        tok_t[...] = tok[0].astype(F32).T.astype(BF)

    def low_fwd():
        low_t[...] = low[...].astype(F32).T.astype(BF)

    st = {}

    def run(name, *a):
        with jax.named_scope(name + "".join("_%d" % i for i in a)):
            OPS[name](*a)

    def start():
        l_tok.wait()
        l_lf.wait()
        lowf[...] = mm(tok[0], lf[...])
        lowp[...] = lowf[...].astype(BF)

    def barrier():
        pl.semaphore_wait(bar, len(peers))

    def low_rs_send():
        st["low"] = scatter(lowp, low_rs)

    def low_ag_send():
        st["low"].got()
        low[pl.ds(t * part, part), :] = gather_sum(lowf, low_rs)
        st["low_ag"] = gather(low)

    def w_low():
        l_rf.wait()
        st["low_ag"].got()

    def w_blk(i):
        l_blk[i].wait()

    def w_z1(i):
        c_z1[i].got()

    def w_xh(k):
        c_xh[k].got()

    def w_z2(k):
        c_z2[NH * k].got(tok.at[3, :, pl.ds(k * kw, kw)])

    def gelu(c):
        if c == 0:
            l_up.wait()
        cs = pl.ds(c * gw, gw)
        last = pl.ds((NK - 1) * kw, kw)
        v = pre[:, cs] + mm(jnp.concatenate([tok[3, :, last], low[...]], 1), jnp.concatenate([blk[3, last, cs], rf[:, cs]], 0))
        u = up[:, cs].astype(F32)
        v2 = v * v
        th = jnp.tanh(v * (C0 + (C0 * C1) * v2))
        g = 0.5 + 0.5 * th
        act[:, cs] = (v * g).astype(BF)
        slope = g + 0.5 * v * (1.0 - th * th) * (C0 + (3.0 * C0 * C1) * v2)
        slo[:, cs] = (u * slope).astype(BF)
        n = NC // NG
        for i in range(c * n, c * n + n):
            rp[i] = mm(low_t[...], slo[:, pl.ds(i * cw, cw)]).astype(BF)
        m = mm_t(slo[:, cs], rf[:, cs])
        if c == 0:
            mixf[...] = m
        else:
            mixf[...] += m
        for i in range(c * n, c * n + n):
            r_pair(i)

    def mix_send():
        mixp[...] = mixf[...].astype(BF)
        st["mix"] = scatter(mixp, mix_rs)

    def mix_ag_send():
        st["mix"].got()
        mix[pl.ds(t * part, part), :] = gather_sum(mixf, mix_rs)
        st["mix_ag"] = gather(mix)

    half, q, e = rank // 2, rank // 8, rank // 16
    g = {}
    up_y, dn_y = dev(xl, yat(1), core), dev(xl, yat(3), core)

    def rgc(c, at, n):
        return rg.at[pl.ds(at, n), pl.ds(c * cw, cw)]

    def rq(c, k, h):
        return pl.ds(yat(k) * q + h * e, e)

    def r_pair(c):
        g["p", c] = send(rp.at[c, pl.ds((1 - core) * half, half)], rpair.at[c], pair)

    def r_s2(c):
        g["p", c].got()
        rps[c] = (rp[c, pl.ds(core * half, half)].astype(F32) + rpair[c].astype(F32)).astype(BF)
        g["yr", c] = Group([(rps.at[c, rq(c, 2, 0)], yrl.at[c, 0], up_y), (rps.at[c, rq(c, 2, 1)], yrl.at[c, 1], dn_y)], yrl.at[c])
        g["yf", c] = Group([(rps.at[c, rq(c, 1, 1)], yfin.at[c, 1], up_y), (rps.at[c, rq(c, 3, 0)], yfin.at[c, 0], dn_y)], yfin.at[c], "y_%d" % c)

    def r_s2b(c):
        g["yr", c].got()
        ybs[c, 0] = (rps[c, rq(c, 1, 0)].astype(F32) + yrl[c, 0].astype(F32)).astype(BF)
        ybs[c, 1] = (rps[c, rq(c, 3, 1)].astype(F32) + yrl[c, 1].astype(F32)).astype(BF)
        g["yb", c] = Group([(ybs.at[c, 0], yb.at[c, 0], up_y), (ybs.at[c, 1], yb.at[c, 1], dn_y)], yb.at[c], "y_%d" % c)

    def r_s3(c):
        g["yf", c].got(rps.at[c, pl.ds(0, 4 * e)])
        for h in range(2):
            total = rps[c, rq(c, 0, h)].astype(F32) + yfin[c, h].astype(F32) + yb[c, h].astype(F32)
            rys[c, pl.ds(h * e, e)] = total.astype(BF)
        g["s3", c] = send(rys.at[c], rxr.at[c], xpeer)

    def r_a2(c):
        g["s3", c].got()
        at = core * half + y * q
        rg[pl.ds(at, q), pl.ds(c * cw, cw)] = ((rys[c].astype(F32) + rxr[c].astype(F32)) * scale).astype(BF)
        here = rgc(c, at, q)
        g["a2", c] = Group([(here, here, up_y), (here, here, dn_y)], rps.at[c, pl.ds(0, 2 * q)])

    def r_a2b(c):
        g["a2", c].got()
        one = rgc(c, core * half + yat(3) * q, e)
        two = rgc(c, core * half + yat(1) * q + e, e)
        g["a2b", c] = Group([(one, one, up_y), (two, two, dn_y)], yb.at[c])

    def r_a3(c):
        g["a2b", c].got()
        here = rgc(c, core * half, half)
        g["a3", c] = send(here, here, pair, "a3")

    def r_end():
        g["a3", 0].got(rg.at[pl.ds(0, half)])

    def gcol(ref, i, k, n=NK):
        w = db // n
        return ref.at[i, :, pl.ds(k * w, w)]

    NX = 6

    def p2(k):
        ks = pl.ds(k * (db // 2), db // 2)
        gs[0, :, ks] = mm_t(slo[...], blk[3, ks, :]).astype(BF)

    def p2_send(k):
        g["g2", k] = send(gcol(gs, 0, k, NX), gcol(gr, 0, k, NX), peer(6), "g2_%d" % (k // 2))

    def px(k):
        ks = pl.ds(k * (db // 2), db // 2)
        gs[1, :, ks] = mm_t(slo[...], blk[1, ks, :]).astype(BF)

    def px_send(k):
        g["gx", k] = send(gcol(gs, 1, k, NX), gcol(gr, 1, k, NX), peer(1), "gx")

    def p1(k):
        ks = pl.ds(k * (db // 2), db // 2)
        pre[:, ks] = mm_t(slo[...], blk[2, ks, :])

    def p1_send(k):
        ks = pl.ds(k * kw, kw)
        g["g2", 2 * k].got(gcol(gr, 0, k))
        gs[2, :, ks] = (pre[:, ks] + gr[0, :, ks].astype(F32)).astype(BF)
        g["g1", k] = send(gcol(gs, 2, k), gcol(gr, 2, k), peer(2), "g1")

    def p0(k):
        ks = pl.ds(k * (db // 2), db // 2)
        own[:, ks] = mm_t(slo[...], blk[0, ks, :])

    lh, le = db // 2, db // 16

    def left():
        st["mix_ag"].got()
        lp[...] = mm(tok_t[...], mix[...]).astype(BF)
        g["lp"] = send(lp.at[pl.ds((1 - core) * lh, lh)], lpair, pair)

    def tg_low():
        own[...] += mm_t(mix[...], lf[...])

    def left_rs():
        g["lp"].got()
        lps[...] = (lp[pl.ds(core * lh, lh)].astype(F32) + lpair[...].astype(F32)).astype(BF)
        cs = []
        for i, (k, f) in enumerate(chips):
            xx = xl if f == 0 else 1 - xl
            cs.append((lps.at[pl.ds(yat(k) * (2 * le) + xx * le, le)], l7r.at[i], chip(k, f)))
        g["l7"] = Group(cs, l7r)

    def left_ag():
        g["l7"].got()
        at = y * (2 * le) + xl * le
        total = lps[pl.ds(at, le)].astype(F32)
        for i in range(7):
            total = total + l7r[i].astype(F32)
        lg[pl.ds(core * lh + at, le)] = (total * scale).astype(BF)
        here = lg.at[pl.ds(core * lh + at, le)]
        g["la"] = Group([(here, here, chip(k, f)) for k, f in chips], l7r)

    def left_pair():
        g["la"].got()
        here = lg.at[pl.ds(core * lh, lh)]
        g["lap"] = send(here, here, pair)

    def left_end():
        g["lap"].got()

    def tg_end():
        g["gx", 0].got(gr.at[1])
        g["g1", 0].got(gr.at[2])
        tg[...] = (own[...] + gr[1].astype(F32) + gr[2].astype(F32)).astype(BF)

    def finish():
        for c in groups:
            c.sent()

    OPS = dict(locals())
    for name, *a in ORDER:
        run(name, *a)
    assert len(slots) == N_RECV


ORDER = [
    ("start",), ("barrier",), ("send_z", 0), ("send_b", 0), ("low_rs_send",), ("send_z", 1), ("send_x", 0), ("send_b", 1),
    *[("send_z", i) for i in range(2, 8)], ("send_x", 1), *[("send_z", i) for i in range(8, 12)], ("send_x", 2), ("own_fwd",),
    ("relay", 0), ("relay_b", 0), ("relay", 1), ("low_ag_send",), ("relay", 2), ("relay_b", 1), ("relay", 3), ("w_blk", 1), ("w_blk", 2),
    ("add_k", 2, 0), ("relay", 4), ("relay", 5), ("w_xh", 0), ("add_k", 1, 0), ("relay", 6), ("relay", 7),
    ("add_k", 2, 1), ("relay", 8), ("relay", 9), ("w_xh", 1), ("add_k", 1, 1), ("w_z1", 10), ("w_z1", 11),
    ("add_k", 2, 2), ("w_blk", 3), ("w_z2", 0), ("add_k", 3, 0), ("w_xh", 2), ("add_k", 1, 2),
    ("w_z2", 1), ("add_k", 3, 1), ("w_low",), ("low_fwd",), ("w_z2", 2),
    ("gelu", 0), ("gelu", 1), ("r_s2", 0), ("r_s2", 1), ("gelu", 2), ("mix_send",), ("r_s2", 2), ("r_s2", 3),
    ("px", 0), ("px_send", 0), ("px_send", 1), ("r_s2", 4), ("r_s2", 5), ("r_s2b", 0), ("r_s2b", 1), ("px", 1), ("r_s2b", 2), ("r_s2b", 3),
    ("p2", 0), ("mix_ag_send",), ("p2_send", 0), ("p2_send", 1), ("r_s2b", 4), ("r_s2b", 5), ("r_s3", 0), ("r_s3", 1), ("p2", 1), ("p2_send", 2),
    ("r_s3", 2), ("r_s3", 3), ("px_send", 2), ("p2_send", 3), ("r_s3", 4), ("r_s3", 5), ("px_send", 3), ("r_a2", 0), ("p2_send", 4), ("left",), ("p2_send", 5), ("r_a2", 1), ("r_a2", 2), ("p1", 0),
    ("r_a2", 3), ("left_rs",), ("p1", 1), ("r_a2b", 0), ("p1_send", 0), ("px_send", 4), ("r_a2", 4), ("r_a2b", 1), ("r_a2", 5), ("p1_send", 1),
    ("px_send", 5), ("p0", 0), ("p1_send", 2), ("r_a2b", 2), ("p0", 1), ("r_a2b", 3), ("r_a3", 0), ("left_ag",), ("tg_low",), ("r_a2b", 4), ("r_a3", 1), ("r_a2b", 5), ("r_a3", 2),
    ("r_a3", 3), ("r_a3", 4), ("left_pair",), ("r_a3", 5), ("tg_end",), ("r_end",), ("left_end",), ("finish",),
]
NB = 10
NH = 4
N_SEND = 20
N_RECV = 70


def move(*refs):
    n = len(refs) // 2
    sem = refs[-1]
    cs = []
    for i in range(n):
        rows = refs[i].shape[0] // CUTS[i]
        for k in range(CUTS[i]):
            at = pl.ds(k * rows, rows)
            cs.append(pltpu.make_async_copy(refs[i].at[at], refs[n + i].at[at], sem.at[len(cs)]))
    for c in cs:
        c.start()
    for c in cs:
        c.wait()


CUTS = (1, 1, 1, 1)


def body(scale, tokens, blocks, left_factor, right_factor, upstream):
    rows, db = tokens.shape
    ns, _, fb = blocks.shape
    rank = left_factor.shape[1]
    cw = fb // NC
    part = rows // 8
    shapes = [
        jax.ShapeDtypeStruct((rows, fb), BF),
        jax.ShapeDtypeStruct((rows, db), BF),
        jax.ShapeDtypeStruct((db, rank), BF),
        jax.ShapeDtypeStruct((rank, fb), BF),
    ]
    V = pltpu.VMEM
    scratch = [
        V((ns, db, fb), BF), V((ns, rows, db), BF), V((db, rows), BF), V((db, rank), BF),
        V((rank, fb), BF), V((rows, fb), BF), V((rows, fb), F32), V((rows, fb), BF),
        V((rows, rank), F32), V((rows, rank), BF), V((7, part, rank), BF), V((rows, rank), BF), V((rank, rows), BF),
        V((rows, rank), F32), V((rows, rank), BF), V((7, part, rank), BF), V((rows, rank), BF),
        V((2, rows // NH, db // NK), BF), V((3, rows, db), BF), V((3, rows, db), BF), V((rows, db), F32),
        V((NC, rank, cw), BF), V((NC, rank // 2, cw), BF), V((NC, rank // 2, cw), BF),
        *[V((NC, 2, rank // 16, cw), BF)] * 4, V((NC, rank // 8, cw), BF), V((NC, rank // 8, cw), BF),
        V((db, rank), BF), V((db // 2, rank), BF), V((db // 2, rank), BF), V((7, db // 16, rank), BF),
        pltpu.SemaphoreType.DMA((8,)), pltpu.SemaphoreType.DMA((N_SEND,)), pltpu.SemaphoreType.DMA((N_RECV,)),
    ]
    any_spec = pl.BlockSpec(memory_space=pl.ANY)
    vmem_spec = pl.BlockSpec(memory_space=pltpu.VMEM)
    res = pl.pallas_call(
        functools.partial(kernel, scale, (rows, db, fb, rank)),
        out_shape=[V(o.shape, o.dtype) for o in shapes],
        in_specs=[any_spec] * 5,
        out_specs=[vmem_spec] * 4,
        scratch_shapes=scratch,
        compiler_params=pltpu.CompilerParams(
            collective_id=0, has_side_effects=True, vmem_limit_bytes=56 * 1024 * 1024
        ),
    )(tokens, blocks, left_factor, right_factor, upstream)
    return pl.pallas_call(
        move,
        out_shape=shapes,
        in_specs=[vmem_spec] * 4,
        out_specs=[any_spec] * 4,
        scratch_shapes=[pltpu.SemaphoreType.DMA((sum(CUTS),))],
        compiler_params=pltpu.CompilerParams(vmem_limit_bytes=1024 * 1024),
    )(*[pltpu.with_memory_space_constraint(r, pltpu.VMEM) for r in res])


def solution(mesh):
    placed = (
        P("dp", "tensor"),
        P(None, "tensor", None),
        P("tensor", None),
        P(None, "tensor"),
        P("dp", "tensor"),
    )

    def whole(tokens, blocks, left_factor, right_factor, upstream):
        scale = 1.0 / float(tokens.shape[0]) ** 0.5
        return jax.shard_map(
            functools.partial(body, scale),
            mesh=mesh,
            in_specs=placed,
            out_specs=(P("dp", "tensor"), P("dp", "tensor"), P("tensor", None), P(None, "tensor")),
            check_vma=False,
        )(tokens, blocks, left_factor, right_factor, upstream)

    return whole
```

```python
import functools

import jax
import jax.numpy as jnp
from jax import lax
from jax.experimental import pallas as pl
from jax.experimental.pallas import tpu as pltpu
from jax.sharding import PartitionSpec as P

MESH = pl.DeviceIdType.MESH
BF = jnp.bfloat16
F32 = jnp.float32
C0 = 0.7978845608028654
C1 = 0.044715

NC = 6
NG = 3
NK = 3


def flip(v, mask):
    for b in range(3):
        if mask >> b & 1:
            bit = lax.rem(lax.div(v, 1 << b), 2)
            v = v + (1 - 2 * bit) * (1 << b)
    return v


def mm(a, b):
    return jnp.dot(a, b, preferred_element_type=F32)


def mm_t(a, b):
    return lax.dot_general(a, b, (((1,), (1,)), ((), ())), preferred_element_type=F32)


def kernel(scale, sizes, tok_h, blk_h, lf_h, rf_h, up_h, act, tg, lg, rg,
           blk, tok, tok_t, lf, rf, up, pre, slo,
           lowf, lowp, low_rs, low, low_t,
           mixf, mixp, mix_rs, mix,
           rb, gs, gr, own,
           rp, rpair, rps, yrl, yfin, ybs, yb, rys, rxr,
           lp, lpair, lps, l7r,
           load_sem, send_sem, recv_sem):
    rows, db, fb, rank = sizes
    cw, kw, gw = fb // NC, db // NK, fb // NG
    part = rows // 8
    d = lax.axis_index("dp")
    t = lax.axis_index("tensor")
    core = lax.rem(d, 2)
    y = lax.rem(lax.div(d, 2), 4)
    xl = lax.div(d, 8)

    def dev(x, yy, c):
        return (x * 8 + yy * 2 + c, t)

    def peer(mask):
        return (d, flip(t, mask))

    def yat(k):
        return lax.rem(y + k, 4)

    pair = dev(xl, y, 1 - core)
    xpeer = dev(1 - xl, y, core)
    chips = [(k, f) for f in range(2) for k in (2, 1, 3, 0) if (k, f) != (0, 0)]

    def chip(k, f):
        return dev(xl if f == 0 else 1 - xl, yat(k), core)

    bar = pltpu.get_barrier_semaphore()
    peers = [peer(m) for m in (7, 5, 6, 4, 3, 1, 2)] + [chip(k, f) for k, f in chips] + [pair]
    for p in peers:
        pl.semaphore_signal(bar, inc=1, device_id=p, device_id_type=MESH)

    loads = []

    def load(src, dst):
        c = pltpu.make_async_copy(src, dst, load_sem.at[len(loads)])
        c.start()
        loads.append(c)
        return c

    l_tok = load(tok_h, tok.at[0])
    l_lf = load(lf_h, lf)
    l_blk = {}
    for i in (0, 2, 1, 3):
        l_blk[i] = load(blk_h.at[i], blk.at[i])
    l_rf = load(rf_h, rf)
    l_up = load(up_h, up)

    groups, slots = [], {}

    class Group:
        def __init__(self, copies, size, key=None):
            n = len(groups)
            if n >= N_SEND:
                groups[n - N_SEND].sent()
            m = slots.setdefault(n if key is None else key, len(slots))
            self.ssem, self.rsem, self.size, self.open = send_sem.at[n % N_SEND], recv_sem.at[m], size, True
            groups.append(self)
            for src, dst, to in copies:
                pltpu.make_async_remote_copy(
                    src_ref=src, dst_ref=dst, send_sem=self.ssem, recv_sem=self.rsem,
                    device_id=to, device_id_type=MESH).start()

        def got(self, size=None):
            size = self.size if size is None else size
            pltpu.make_async_copy(size, size, self.rsem).wait()

        def sent(self):
            if self.open:
                pltpu.make_async_copy(self.size, self.size, self.ssem).wait()
                self.open = False

    def send(src, dst, to, key=None):
        return Group([(src, dst, to)], dst, key)

    def scatter(src, dst):
        return Group([(src.at[pl.ds(flip(t, m) * part, part)], dst.at[m - 1], peer(m)) for m in (7, 5, 6, 4, 3, 1, 2)], dst)

    def gather(buf):
        here = buf.at[pl.ds(t * part, part)]
        return Group([(here, here, peer(m)) for m in (7, 5, 6, 4, 3, 1, 2)], buf.at[pl.ds(0, 7 * part)])

    def gather_sum(f32_ref, recv):
        total = f32_ref[pl.ds(t * part, part), :]
        for m in range(7):
            total = total + recv[m].astype(F32)
        return total.astype(BF)

    def col(c):
        return pl.ds(pl.multiple_of(c * cw, cw), cw)

    def add_k(s, k):
        ks = pl.ds(k * kw, kw)

        def step(c, _):
            pre[:, col(c)] += mm(tok[s, :, ks], blk[s, ks, col(c)])
            return 0

        lax.fori_loop(0, NC, step, 0, unroll=True)

    hr = rows // NH
    quads = [(k, h) for k in range(NK) for h in range(NH)]

    def piece(s, k, h):
        return tok.at[s, pl.ds(h * hr, hr), pl.ds(k * kw, kw)]

    c_z1, c_xh, c_z2, c_b, c_z2b = [], [], [], [], []

    def send_z(i):
        k, h = quads[i]
        c_z1.append(send(tok_h.at[pl.ds(h * hr, hr), pl.ds(k * kw, kw)], piece(2, k, h), peer(2)))

    def send_x(k):
        ks = pl.ds(k * kw, kw)
        c_xh.append(send(tok_h.at[:, ks], tok.at[1, :, ks], peer(1)))

    def send_b(j):
        k, h = quads[NB + j]
        c_b.append(send(tok_h.at[pl.ds(h * hr, hr), pl.ds(k * kw, kw)], rb.at[j], peer(6)))

    def relay_b(j):
        k, h = quads[NB + j]
        c_b[j].got()
        c_z2b.append(send(rb.at[j], piece(3, k, h), peer(2), "z2_%d" % k))

    def relay(i):
        k, h = quads[i]
        c_z1[i].got()
        c_z2.append(send(piece(2, k, h), piece(3, k, h), peer(6), "z2_%d" % k))

    def own_fwd():
        l_blk[0].wait()

        def step(c, _):
            pre[:, col(c)] = mm(tok[0], blk[0, :, col(c)])
            return 0

        lax.fori_loop(0, NC, step, 0, unroll=True)
        tok_t[...] = tok[0].astype(F32).T.astype(BF)

    def low_fwd():
        low_t[...] = low[...].astype(F32).T.astype(BF)

    st = {}

    def run(name, *a):
        with jax.named_scope(name + "".join("_%d" % i for i in a)):
            OPS[name](*a)

    def start():
        l_tok.wait()
        l_lf.wait()
        lowf[...] = mm(tok[0], lf[...])
        lowp[...] = lowf[...].astype(BF)

    def barrier():
        pl.semaphore_wait(bar, len(peers))

    def low_rs_send():
        st["low"] = scatter(lowp, low_rs)

    def low_ag_send():
        st["low"].got()
        low[pl.ds(t * part, part), :] = gather_sum(lowf, low_rs)
        st["low_ag"] = gather(low)

    def w_low():
        l_rf.wait()
        st["low_ag"].got()

    def w_blk(i):
        l_blk[i].wait()

    def w_z1(i):
        c_z1[i].got()

    def w_xh(k):
        c_xh[k].got()

    def w_z2(k):
        c_z2[NH * k].got(tok.at[3, :, pl.ds(k * kw, kw)])

    def gelu(c):
        if c == 0:
            l_up.wait()
        cs = pl.ds(c * gw, gw)
        last = pl.ds((NK - 1) * kw, kw)
        v = pre[:, cs] + mm(jnp.concatenate([tok[3, :, last], low[...]], 1), jnp.concatenate([blk[3, last, cs], rf[:, cs]], 0))
        u = up[:, cs].astype(F32)
        v2 = v * v
        th = jnp.tanh(v * (C0 + (C0 * C1) * v2))
        g = 0.5 + 0.5 * th
        act[:, cs] = (v * g).astype(BF)
        slope = g + 0.5 * v * (1.0 - th * th) * (C0 + (3.0 * C0 * C1) * v2)
        slo[:, cs] = (u * slope).astype(BF)
        n = NC // NG
        for i in range(c * n, c * n + n):
            rp[i] = mm(low_t[...], slo[:, pl.ds(i * cw, cw)]).astype(BF)
        m = mm_t(slo[:, cs], rf[:, cs])
        if c == 0:
            mixf[...] = m
        else:
            mixf[...] += m
        for i in range(c * n, c * n + n):
            r_pair(i)

    def mix_send():
        mixp[...] = mixf[...].astype(BF)
        st["mix"] = scatter(mixp, mix_rs)

    def mix_ag_send():
        st["mix"].got()
        mix[pl.ds(t * part, part), :] = gather_sum(mixf, mix_rs)
        st["mix_ag"] = gather(mix)

    half, q, e = rank // 2, rank // 8, rank // 16
    g = {}
    up_y, dn_y = dev(xl, yat(1), core), dev(xl, yat(3), core)

    def rgc(c, at, n):
        return rg.at[pl.ds(at, n), pl.ds(c * cw, cw)]

    def rq(c, k, h):
        return pl.ds(yat(k) * q + h * e, e)

    def r_pair(c):
        g["p", c] = send(rp.at[c, pl.ds((1 - core) * half, half)], rpair.at[c], pair)

    def r_s2(c):
        g["p", c].got()
        rps[c] = (rp[c, pl.ds(core * half, half)].astype(F32) + rpair[c].astype(F32)).astype(BF)
        g["yr", c] = Group([(rps.at[c, rq(c, 2, 0)], yrl.at[c, 0], up_y), (rps.at[c, rq(c, 2, 1)], yrl.at[c, 1], dn_y)], yrl.at[c])
        g["yf", c] = Group([(rps.at[c, rq(c, 1, 1)], yfin.at[c, 1], up_y), (rps.at[c, rq(c, 3, 0)], yfin.at[c, 0], dn_y)], yfin.at[c], "y_%d" % c)

    def r_s2b(c):
        g["yr", c].got()
        ybs[c, 0] = (rps[c, rq(c, 1, 0)].astype(F32) + yrl[c, 0].astype(F32)).astype(BF)
        ybs[c, 1] = (rps[c, rq(c, 3, 1)].astype(F32) + yrl[c, 1].astype(F32)).astype(BF)
        g["yb", c] = Group([(ybs.at[c, 0], yb.at[c, 0], up_y), (ybs.at[c, 1], yb.at[c, 1], dn_y)], yb.at[c], "y_%d" % c)

    def r_s3(c):
        g["yf", c].got(rps.at[c, pl.ds(0, 4 * e)])
        for h in range(2):
            total = rps[c, rq(c, 0, h)].astype(F32) + yfin[c, h].astype(F32) + yb[c, h].astype(F32)
            rys[c, pl.ds(h * e, e)] = total.astype(BF)
        g["s3", c] = send(rys.at[c], rxr.at[c], xpeer)

    def r_a2(c):
        g["s3", c].got()
        at = core * half + y * q
        rg[pl.ds(at, q), pl.ds(c * cw, cw)] = ((rys[c].astype(F32) + rxr[c].astype(F32)) * scale).astype(BF)
        here = rgc(c, at, q)
        g["a2", c] = Group([(here, here, up_y), (here, here, dn_y)], rps.at[c, pl.ds(0, 2 * q)])

    def r_a2b(c):
        g["a2", c].got()
        one = rgc(c, core * half + yat(3) * q, e)
        two = rgc(c, core * half + yat(1) * q + e, e)
        g["a2b", c] = Group([(one, one, up_y), (two, two, dn_y)], yb.at[c])

    def r_a3(c):
        g["a2b", c].got()
        here = rgc(c, core * half, half)
        g["a3", c] = send(here, here, pair, "a3")

    def r_end():
        g["a3", 0].got(rg.at[pl.ds(0, half)])

    def gcol(ref, i, k, n=NK):
        w = db // n
        return ref.at[i, :, pl.ds(k * w, w)]

    NX = 6

    def p2(k):
        ks = pl.ds(k * (db // 2), db // 2)
        gs[0, :, ks] = mm_t(slo[...], blk[3, ks, :]).astype(BF)

    def p2_send(k):
        g["g2", k] = send(gcol(gs, 0, k, NX), gcol(gr, 0, k, NX), peer(6), "g2_%d" % (k // 2))

    def px(k):
        ks = pl.ds(k * (db // 2), db // 2)
        gs[1, :, ks] = mm_t(slo[...], blk[1, ks, :]).astype(BF)

    def px_send(k):
        g["gx", k] = send(gcol(gs, 1, k, NX), gcol(gr, 1, k, NX), peer(1), "gx")

    def p1(k):
        ks = pl.ds(k * (db // 2), db // 2)
        pre[:, ks] = mm_t(slo[...], blk[2, ks, :])

    def p1_send(k):
        ks = pl.ds(k * kw, kw)
        g["g2", 2 * k].got(gcol(gr, 0, k))
        gs[2, :, ks] = (pre[:, ks] + gr[0, :, ks].astype(F32)).astype(BF)
        g["g1", k] = send(gcol(gs, 2, k), gcol(gr, 2, k), peer(2), "g1")

    def p0(k):
        ks = pl.ds(k * (db // 2), db // 2)
        own[:, ks] = mm_t(slo[...], blk[0, ks, :])

    lh, le = db // 2, db // 16

    def left():
        st["mix_ag"].got()
        lp[...] = mm(tok_t[...], mix[...]).astype(BF)
        g["lp"] = send(lp.at[pl.ds((1 - core) * lh, lh)], lpair, pair)

    def tg_low():
        own[...] += mm_t(mix[...], lf[...])

    def left_rs():
        g["lp"].got()
        lps[...] = (lp[pl.ds(core * lh, lh)].astype(F32) + lpair[...].astype(F32)).astype(BF)
        cs = []
        for i, (k, f) in enumerate(chips):
            xx = xl if f == 0 else 1 - xl
            cs.append((lps.at[pl.ds(yat(k) * (2 * le) + xx * le, le)], l7r.at[i], chip(k, f)))
        g["l7"] = Group(cs, l7r)

    def left_ag():
        g["l7"].got()
        at = y * (2 * le) + xl * le
        total = lps[pl.ds(at, le)].astype(F32)
        for i in range(7):
            total = total + l7r[i].astype(F32)
        lg[pl.ds(core * lh + at, le)] = (total * scale).astype(BF)
        here = lg.at[pl.ds(core * lh + at, le)]
        g["la"] = Group([(here, here, chip(k, f)) for k, f in chips], l7r)

    def left_pair():
        g["la"].got()
        here = lg.at[pl.ds(core * lh, lh)]
        g["lap"] = send(here, here, pair)

    def left_end():
        g["lap"].got()

    def tg_end():
        g["gx", 0].got(gr.at[1])
        g["g1", 0].got(gr.at[2])
        tg[...] = (own[...] + gr[1].astype(F32) + gr[2].astype(F32)).astype(BF)

    def finish():
        for c in groups:
            c.sent()

    OPS = dict(locals())
    for name, *a in ORDER:
        run(name, *a)
    assert len(slots) == N_RECV


ORDER = [
    ("barrier",), ("send_z", 0), ("send_b", 0), ("start",), ("low_rs_send",), ("send_z", 1), ("send_x", 0), ("send_b", 1),
    *[("send_z", i) for i in range(2, 8)], ("send_x", 1), *[("send_z", i) for i in range(8, 12)], ("send_x", 2), ("own_fwd",),
    ("relay", 0), ("relay_b", 0), ("relay", 1), ("low_ag_send",), ("relay", 2), ("relay_b", 1), ("relay", 3), ("w_blk", 1), ("w_blk", 2),
    ("add_k", 2, 0), ("relay", 4), ("relay", 5), ("w_xh", 0), ("add_k", 1, 0), ("relay", 6), ("relay", 7),
    ("add_k", 2, 1), ("relay", 8), ("relay", 9), ("w_xh", 1), ("add_k", 1, 1), ("w_z1", 10), ("w_z1", 11),
    ("add_k", 2, 2), ("w_blk", 3), ("w_z2", 0), ("add_k", 3, 0), ("w_xh", 2), ("add_k", 1, 2),
    ("w_z2", 1), ("add_k", 3, 1), ("w_low",), ("low_fwd",), ("w_z2", 2),
    ("gelu", 0), ("gelu", 1), ("r_s2", 0), ("r_s2", 1), ("gelu", 2), ("mix_send",), ("r_s2", 2), ("r_s2", 3),
    ("px", 0), ("px_send", 0), ("px_send", 1), ("r_s2", 4), ("r_s2", 5), ("r_s2b", 0), ("r_s2b", 1), ("px", 1), ("r_s2b", 2), ("r_s2b", 3),
    ("p2", 0), ("mix_ag_send",), ("p2_send", 0), ("p2_send", 1), ("r_s2b", 4), ("r_s2b", 5), ("r_s3", 0), ("r_s3", 1), ("p2", 1), ("p2_send", 2),
    ("r_s3", 2), ("r_s3", 3), ("px_send", 2), ("p2_send", 3), ("r_s3", 4), ("r_s3", 5), ("r_a2", 0), ("p2_send", 4), ("left",), ("p2_send", 5), ("r_a2", 1), ("r_a2", 2), ("px_send", 3), ("p1", 0),
    ("r_a2", 3), ("left_rs",), ("p1", 1), ("r_a2b", 0), ("p1_send", 0), ("px_send", 4), ("r_a2", 4), ("r_a2b", 1), ("r_a2", 5), ("p1_send", 1),
    ("px_send", 5), ("p0", 0), ("p1_send", 2), ("r_a2b", 2), ("p0", 1), ("r_a2b", 3), ("r_a3", 0), ("left_ag",), ("tg_low",), ("r_a2b", 4), ("r_a3", 1), ("r_a2b", 5), ("r_a3", 2),
    ("r_a3", 3), ("r_a3", 4), ("left_pair",), ("r_a3", 5), ("tg_end",), ("r_end",), ("left_end",), ("finish",),
]
NB = 10
NH = 4
N_SEND = 20
N_RECV = 70


def move(*refs):
    n = len(refs) // 2
    sem = refs[-1]
    cs = []
    for i in range(n):
        rows = refs[i].shape[0] // CUTS[i]
        for k in range(CUTS[i]):
            at = pl.ds(k * rows, rows)
            cs.append(pltpu.make_async_copy(refs[i].at[at], refs[n + i].at[at], sem.at[len(cs)]))
    for c in cs:
        c.start()
    for c in cs:
        c.wait()


CUTS = (1, 1, 1, 1)


def body(scale, tokens, blocks, left_factor, right_factor, upstream):
    rows, db = tokens.shape
    ns, _, fb = blocks.shape
    rank = left_factor.shape[1]
    cw = fb // NC
    part = rows // 8
    shapes = [
        jax.ShapeDtypeStruct((rows, fb), BF),
        jax.ShapeDtypeStruct((rows, db), BF),
        jax.ShapeDtypeStruct((db, rank), BF),
        jax.ShapeDtypeStruct((rank, fb), BF),
    ]
    V = pltpu.VMEM
    scratch = [
        V((ns, db, fb), BF), V((ns, rows, db), BF), V((db, rows), BF), V((db, rank), BF),
        V((rank, fb), BF), V((rows, fb), BF), V((rows, fb), F32), V((rows, fb), BF),
        V((rows, rank), F32), V((rows, rank), BF), V((7, part, rank), BF), V((rows, rank), BF), V((rank, rows), BF),
        V((rows, rank), F32), V((rows, rank), BF), V((7, part, rank), BF), V((rows, rank), BF),
        V((2, rows // NH, db // NK), BF), V((3, rows, db), BF), V((3, rows, db), BF), V((rows, db), F32),
        V((NC, rank, cw), BF), V((NC, rank // 2, cw), BF), V((NC, rank // 2, cw), BF),
        *[V((NC, 2, rank // 16, cw), BF)] * 4, V((NC, rank // 8, cw), BF), V((NC, rank // 8, cw), BF),
        V((db, rank), BF), V((db // 2, rank), BF), V((db // 2, rank), BF), V((7, db // 16, rank), BF),
        pltpu.SemaphoreType.DMA((8,)), pltpu.SemaphoreType.DMA((N_SEND,)), pltpu.SemaphoreType.DMA((N_RECV,)),
    ]
    any_spec = pl.BlockSpec(memory_space=pl.ANY)
    vmem_spec = pl.BlockSpec(memory_space=pltpu.VMEM)
    res = pl.pallas_call(
        functools.partial(kernel, scale, (rows, db, fb, rank)),
        out_shape=[V(o.shape, o.dtype) for o in shapes],
        in_specs=[any_spec] * 5,
        out_specs=[vmem_spec] * 4,
        scratch_shapes=scratch,
        compiler_params=pltpu.CompilerParams(
            collective_id=0, has_side_effects=True, vmem_limit_bytes=56 * 1024 * 1024
        ),
    )(tokens, blocks, left_factor, right_factor, upstream)
    return pl.pallas_call(
        move,
        out_shape=shapes,
        in_specs=[vmem_spec] * 4,
        out_specs=[any_spec] * 4,
        scratch_shapes=[pltpu.SemaphoreType.DMA((sum(CUTS),))],
        compiler_params=pltpu.CompilerParams(vmem_limit_bytes=1024 * 1024),
    )(*[pltpu.with_memory_space_constraint(r, pltpu.VMEM) for r in res])


def solution(mesh):
    placed = (
        P("dp", "tensor"),
        P(None, "tensor", None),
        P("tensor", None),
        P(None, "tensor"),
        P("dp", "tensor"),
    )

    def whole(tokens, blocks, left_factor, right_factor, upstream):
        scale = 1.0 / float(tokens.shape[0]) ** 0.5
        return jax.shard_map(
            functools.partial(body, scale),
            mesh=mesh,
            in_specs=placed,
            out_specs=(P("dp", "tensor"), P("dp", "tensor"), P("tensor", None), P(None, "tensor")),
            check_vma=False,
        )(tokens, blocks, left_factor, right_factor, upstream)

    return whole
```
